256 devices in a mesh: grp: 8 (over x_lo, y), shard: 32 (over x_hi, z, core).
Axes of the slice: x: 4 (x_hi: 2, x_lo: 2; x = x_hi * 2 + x_lo), y: 4, z: 8, core: 2. Of those that a mesh axis runs over, the one named last changes fastest.
Arguments:
- hidden_acts: bfloat16 [16384, 16384], P('shard', 'grp'), may hold values from -6 to 6
- cotangent: bfloat16 [16384, 5120], P('shard'), may hold values from -0.09375 to 0.09375
- master: float32 [5120, 16384], P('shard', 'grp'), may hold values from -0.046875 to 0.046875
- moment_one: float32 [5120, 16384], P('shard', 'grp'), may hold values from -3 to 3
- moment_two: float32 [5120, 16384], P('shard', 'grp'), may hold values from 0.01 to 1
- held_bucket: int32 [8], replicated, may hold values from 0 to 7, each once
- decode_in: bfloat16 [1024, 16384], P('grp', 'shard'), may hold values from -6 to 6
Outputs:
- master_new: float32 [5120, 16384], P('shard', 'grp')
- moment_one_new: float32 [5120, 16384], P('shard', 'grp')
- moment_two_new: float32 [5120, 16384], P('shard', 'grp')
- decode_out: bfloat16 [1024, 5120], P('grp', 'shard')
The draws below stay inside these ranges and needn't reach their ends.
Inputs may be any that keep to these rules, and one draw needn't show every extreme that they name: held_bucket names each of the 8 buckets exactly once.
All inputs are finite; a program needn't handle non-finite values.
Results may differ from the reference program's by a relative error of at most 0.025.
Values may be sent and summed in bfloat16 or wider, within the bound.
A program may use at most 256 MiB of HBM per device.

```python
import math
import jax
import jax.numpy as jnp
from jax import lax

D = 5120
FFW = 16384
TOK_DEV = 512
ROWS = 128
TOKENS = 16384
N_GRP = 8
N_SHARD = 32


def spiked(drawn, stream_key, source, target, shards_of, factor):
    owner, partner = [(jnp.arange(drawn.shape[axis_at]) // (drawn.shape[axis_at] // shards_of)).reshape([-1 if axis == axis_at else 1 for axis in range(drawn.ndim)]) for axis_at in (source, target)]
    chosen = jax.random.permutation(stream_key, shards_of)[partner]
    strong = (owner == chosen) | (owner == (partner + shards_of // 2) % shards_of)
    return jnp.where(strong, factor * drawn, drawn)


def block_scale(rng, extent, split, least, largest):
    factor_of, own = 1.0, jax.random.fold_in(rng, 6)
    for position, parts in split:
        draws = jnp.exp(jax.random.uniform(jax.random.fold_in(own, position), (parts,), jnp.float32, least / len(split), largest / len(split)))
        factor_of = factor_of * jnp.repeat(draws, extent[position] // parts).reshape([-1 if axis == position else 1 for axis in range(len(extent))])
    return factor_of


def normal_values(key, shape, spread, reach, cuts=(), dtype=jnp.bfloat16):
    entries = jax.random.normal(key, shape, jnp.float32) * spread
    if len(cuts) > 0:
        entries = block_scale(key, shape, cuts, -0.22, 0.18) * entries
    return jnp.clip(entries, min=-reach, max=reach).astype(dtype)


def heavy_noise(key, dims, scale, bound, shards, heavy, held_as=jnp.bfloat16):
    entries = scale * jax.random.normal(key, dims, jnp.float32)
    if shards:
        entries = entries * block_scale(key, dims, shards, -0.22, 0.18)
    return jnp.clip(spiked(entries, jax.random.fold_in(key, 3), *heavy), -bound, bound).astype(held_as)


def setup_inputs(seed: int = 0) -> dict:
    arg_keys = jax.random.split(jax.random.key(seed), 8)
    hidden_acts = normal_values(arg_keys[0], (TOKENS, FFW), 1.0, 6.0, ((0, 32), (1, 8)))
    cotangent = heavy_noise(arg_keys[1], (TOKENS, D), (TOKENS ** -0.5), 0.09375, ((0, 32),), (0, 1, 32, 2.75))
    master = normal_values(arg_keys[2], (D, FFW), FFW ** -0.5, 0.046875, ((0, 32), (1, 8)), jnp.float32)
    moment_one = normal_values(arg_keys[3], (D, FFW), 0.3, 3.0, ((0, 32), (1, 8)), jnp.float32)
    moment_two = jnp.clip(jnp.exp(math.log(1.0) - 4.6051702 * jax.random.uniform(arg_keys[4], (D, FFW), jnp.float32) ** block_scale(arg_keys[4], (D, FFW), ((0, 32), (1, 8)), -0.2, 0.2)), 0.01, 1.0)
    held_bucket = jax.random.permutation(arg_keys[5], N_GRP).astype(jnp.int32)
    decode_in = normal_values(arg_keys[6], (N_GRP * ROWS, FFW), 1.0, 6.0, ((0, 8), (1, 32)))
    return {"hidden_acts": hidden_acts, "cotangent": cotangent, "master": master, "moment_one": moment_one, "moment_two": moment_two, "held_bucket": held_bucket, "decode_in": decode_in}


beta_one = 0.9
beta_two = 0.95
learn_rate = 0.001
decay_rate = 0.1
epsilon = 1e-08
correct_one = 1.0 - 0.9 ** 50
correct_two = 1.0 - 0.95 ** 50

def reference(hidden_acts, cotangent, master, moment_one, moment_two, held_bucket, decode_in):
    acts_split = hidden_acts.reshape(N_SHARD, TOK_DEV, FFW)
    cots_split = cotangent.reshape(N_SHARD, TOK_DEV, D)

    def add_partial(running, pair):
        partial_value = jnp.dot(pair[1].T, pair[0], preferred_element_type=jnp.float32)
        partial_value = lax.optimization_barrier(partial_value.astype(jnp.bfloat16)).astype(jnp.float32)
        return (running + partial_value, None)
    gradient, _ = lax.scan(add_partial, jnp.zeros((D, FFW), jnp.float32), (acts_split, cots_split))
    moment_one_new = beta_one * moment_one + (1.0 - beta_one) * gradient
    moment_two_new = beta_two * moment_two + (1.0 - beta_two) * gradient * gradient
    update = moment_one_new / correct_one / (jnp.sqrt(moment_two_new / correct_two) + epsilon)
    master_new = master - learn_rate * (update + decay_rate * master)
    weights = master_new.astype(jnp.bfloat16)
    total_rows = decode_in.shape[0]
    blocks = decode_in.reshape(total_rows, N_GRP, FFW // N_GRP)
    picked = jnp.take(blocks, held_bucket, axis=1).reshape(total_rows, FFW)
    decode_out = jnp.dot(picked, weights.T, preferred_element_type=jnp.float32).astype(jnp.bfloat16)
    return (master_new, moment_one_new, moment_two_new, decode_out)
```

```python
import jax
import jax.numpy as jnp
from jax import lax
from jax.experimental import pallas as pl
from jax.experimental.pallas import tpu as pltpu
from jax.sharding import PartitionSpec as P

beta_one = 0.9
beta_two = 0.95
learn_rate = 0.001
decay_rate = 0.1
epsilon = 1e-08
correct_one = 1.0 - 0.9**50
correct_two = 1.0 - 0.95**50

NX, NY, NZ = 4, 4, 8
FEAT = 5120
HALF = FEAT // 2
OWN = 160
CHIP = 2 * OWN
TOK = 512
BUCKET = 2048
COLS = BUCKET // 2
WAVES = 4
WCOL = COLS // WAVES
LANE = WCOL // 2
PIECES = 4
PCOL = HALF // PIECES
PROW = TOK // NY
ROWS = 128
DCOL = 512
LAG = 2
LAST = 11


def aligned(value, step):
    return pl.multiple_of(value, step)


def device_at(x, y, z, core):
    x, y, z = lax.rem(x, NX), lax.rem(y, NY), lax.rem(z, NZ)
    return {
        "grp": lax.rem(x, 2) * NY + y,
        "shard": (x // 2) * 16 + z * 2 + core,
    }


def kernel(
    hid, cot, master, mom_one, mom_two, held, dec,
    master_out, one_out, two_out, dec_out,
    cotv, hidv, pv, rv, gx, st, wv, xv, acc,
    local_sem, in_send, in_recv,
    cc_send, cc_recv, cy_send, cy_recv, cf_send, cf_recv, cs_send, cs_recv,
    hx_send, hx_recv, xx_send, xx_recv, xz_send, xz_recv, xs_send, xs_recv,
    r_send, r_recv, g_send, g_recv,
    ax_send, ax_recv, ay_send, ay_recv, af_send, af_recv, out_sem,
):
    grp = lax.axis_index("grp")
    shard = lax.axis_index("shard")
    x_lo, y = grp // NY, lax.rem(grp, NY)
    x_hi, z, core = shard // 16, lax.rem(shard, 16) // 2, lax.rem(shard, 2)
    x = x_hi * 2 + x_lo
    other = 1 - core

    sibling = device_at(x, y, z, other)
    z_up, z_down = device_at(x, y, z + 1, core), device_at(x, y, z + NZ - 1, core)
    y_up, y_down = device_at(x, y + 1, z, core), device_at(x, y + NY - 1, z, core)
    x_half = device_at(x + 2, y, z, core)
    x_half_other = device_at(x + 2, y, z, other)
    x_cross = device_at(3 - x, y, z, core)
    x_pair = device_at(x_hi * 2 + 1 - x_lo, y, z, core)
    z_way = (z_up, z_down)
    y_way = (y_up, y_down)

    def remote(src, dst, send, recv, device):
        return pltpu.make_async_remote_copy(
            src_ref=src, dst_ref=dst, send_sem=send, recv_sem=recv,
            device_id=device, device_id_type=pl.DeviceIdType.MESH,
        )

    barrier = pltpu.get_barrier_semaphore()
    partners = (
        sibling, z_up, z_down, y_up, y_down, x_half, x_half_other, x_cross, x_pair,
    )
    for partner in partners:
        pl.semaphore_signal(
            barrier, inc=1, device_id=partner, device_id_type=pl.DeviceIdType.MESH
        )

    mine = pl.ds(aligned(core * TOK, TOK), TOK)
    loads = [
        pltpu.make_async_copy(
            cot.at[:, pl.ds(aligned(x_hi * HALF, HALF), HALF)], cotv.at[mine, :],
            local_sem.at[0],
        ),
        pltpu.make_async_copy(
            hid.at[:, pl.ds(aligned(core * COLS, COLS), COLS)], hidv.at[mine, :],
            local_sem.at[1],
        ),
        pltpu.make_async_copy(
            dec, xv.at[shard], local_sem.at[2]
        ),
        pltpu.make_async_copy(master, st.at[0], local_sem.at[3]),
        pltpu.make_async_copy(mom_one, st.at[1], local_sem.at[4]),
        pltpu.make_async_copy(mom_two, st.at[2], local_sem.at[5]),
    ]
    for copy in loads:
        copy.start()

    def cot_sibling():
        return remote(
            cot.at[:, pl.ds(aligned(x_hi * HALF, HALF), HALF)], cotv.at[mine, :],
            in_send.at[0], in_recv.at[0], sibling,
        )

    def hid_sibling():
        return remote(
            hid.at[:, pl.ds(aligned(other * COLS, COLS), COLS)], hidv.at[mine, :],
            in_send.at[1], in_recv.at[1], sibling,
        )

    def cot_rows(owner, first, count):
        return pl.ds(aligned((2 + core) * TOK + owner * PROW + first, 64), count)

    def cot_cols(piece):
        return pl.ds(aligned(piece * PCOL, PCOL), PCOL)

    def cot_cross(piece):
        return remote(
            cot.at[
                pl.ds(aligned(y * PROW, PROW), PROW),
                pl.ds(aligned((1 - x_hi) * HALF + piece * PCOL, 128), PCOL),
            ],
            cotv.at[cot_rows(y, 0, PROW), cot_cols(piece)],
            cc_send.at[piece], cc_recv.at[piece], x_cross,
        )

    def cot_y(way, piece):
        part = cotv.at[cot_rows(y, 0, PROW), cot_cols(piece)]
        return remote(
            part, part, cy_send.at[way, piece], cy_recv.at[way, piece], y_way[way]
        )

    def cot_forward(way, piece):
        owner = lax.rem(y + (NY - 1 if way == 0 else 1), NY)
        part = cotv.at[cot_rows(owner, way * (PROW // 2), PROW // 2), cot_cols(piece)]
        return remote(
            part, part, cf_send.at[way, piece], cf_recv.at[way, piece], y_way[way]
        )

    def cot_share(which, piece):
        owner = lax.rem(y + (0, NY - 1, 1, 2)[which], NY)
        part = cotv.at[cot_rows(owner, 0, PROW), cot_cols(piece)]
        return remote(
            part, part, cs_send.at[which, piece], cs_recv.at[which, piece], sibling
        )

    def wave_cols(wave):
        return pl.ds(aligned(wave * WCOL, WCOL), WCOL)

    def hid_half(wave, target):
        rows = pl.ds(aligned((2 + core) * TOK, TOK), TOK)
        device = device_at(x + 2, y, z, target)
        return remote(
            hid.at[:, pl.ds(aligned(target * COLS + wave * WCOL, WCOL), WCOL)],
            hidv.at[rows, wave_cols(wave)],
            hx_send.at[wave, target], hx_recv.at[wave, core], device,
        )

    def hid_half_wait(wave, source):
        part = hidv.at[pl.ds((2 + source) * TOK, TOK), wave_cols(wave)]
        pltpu.make_async_copy(part, part, hx_recv.at[wave, source]).wait()

    def dec_index(half, place):
        return half * 16 + place * 2 + core

    def dec_half():
        return remote(
            dec, xv.at[shard],
            xx_send.at[0], xx_recv.at[0], x_half,
        )

    def dec_z(part, way, step):
        half = x_hi if part == 0 else 1 - x_hi
        place = lax.rem(z + (NZ - step if way == 0 else step), NZ)
        rows = pl.ds(0, ROWS)
        if step == 3:
            rows = pl.ds(way * (ROWS // 2), ROWS // 2)
        block = xv.at[dec_index(half, place), rows]
        return remote(
            block, block, xz_send.at[part, way, step], xz_recv.at[part, way, step],
            z_way[way],
        )

    def dec_share(part, slot):
        half = x_hi if part == 0 else 1 - x_hi
        shift = (NZ - 1, NZ - 2, NZ - 3, 1, 2, 3, 4, 0)[slot]
        block = xv.at[dec_index(half, lax.rem(z + shift, NZ))]
        return remote(
            block, block, xs_send.at[part, slot], xs_recv.at[part, slot], sibling
        )

    def ring_block(way, step):
        if way == 0:
            return lax.rem(z + 2 * NZ - 1 - step, NZ)
        return lax.rem(z + 1 + step, NZ)

    def ring_rows(place):
        return pl.ds(aligned(place * CHIP, CHIP), CHIP)

    def ring_first(wave, way):
        return remote(
            pv.at[wave, ring_rows(ring_block(way, 0)), pl.ds(way * LANE, LANE)],
            rv.at[wave, way, 0],
            r_send.at[wave, way, 0], r_recv.at[wave, way, 0], z_way[way],
        )

    def ring_next(wave, way, step):
        return remote(
            rv.at[wave, way, step - 1], rv.at[wave, way, step],
            r_send.at[wave, way, step], r_recv.at[wave, way, step], z_way[way],
        )

    def chip_rows(which):
        return pl.ds(aligned(z * CHIP + which * OWN, 32), OWN)

    def grad_swap(wave):
        return remote(
            pv.at[wave, chip_rows(other), :], gx.at[wave],
            g_send.at[wave], g_recv.at[wave], sibling,
        )

    def weights_pair(wave):
        block = wv.at[grp, wave]
        return remote(block, block, ax_send.at[wave], ax_recv.at[wave], x_pair)

    def weights_y(wave, part, way):
        side = x_lo if part == 0 else 1 - x_lo
        block = wv.at[side * NY + y, wave]
        return remote(
            block, block, ay_send.at[wave, part, way], ay_recv.at[wave, part, way],
            y_way[way],
        )

    def weights_forward(wave, part, way):
        side = x_lo if part == 0 else 1 - x_lo
        owner = lax.rem(y + (NY - 1 if way == 0 else 1), NY)
        block = wv.at[side * NY + owner, wave, pl.ds(way * (OWN // 2), OWN // 2), :]
        return remote(
            block, block, af_send.at[wave, part, way], af_recv.at[wave, part, way],
            y_way[way],
        )

    def state_cols(wave, half):
        return pl.ds(aligned(half * COLS + wave * WCOL, WCOL), WCOL)

    def store_out(wave, half, which):
        cols = state_cols(wave, half)
        target = (master_out, one_out, two_out)[which]
        return pltpu.make_async_copy(
            st.at[which, :, cols], target.at[:, cols], out_sem.at[wave, half, which]
        )

    pl.semaphore_wait(barrier, len(partners))
    for piece in range(PIECES):
        cot_cross(piece).start()
    dec_half().start()
    loads[2].wait()
    for way in range(2):
        dec_z(0, way, 0).start()
    dec_share(0, 7).start()
    cot_sibling().start()
    hid_sibling().start()

    for piece in range(PIECES):
        cot_cross(piece).wait_recv()
        for way in range(2):
            cot_y(way, piece).start()
        cot_share(0, piece).start()
        if piece == 0:
            dec_half().wait_recv()
            for way in range(2):
                dec_z(1, way, 0).start()
            dec_share(1, 7).start()
        if piece == 1:
            for target in range(2):
                hid_half(0, target).start()
    for wave in range(1, WAVES):
        for target in range(2):
            hid_half(wave, target).start()

    for piece in range(PIECES):
        for way in range(2):
            cot_y(way, piece).wait_recv()
            cot_forward(way, piece).start()
            cot_share(1 + way, piece).start()
        if piece < 3:
            for part in range(2):
                for way in range(2):
                    dec_z(part, way, piece).wait_recv()
                    dec_z(part, way, piece + 1).start()
                    dec_share(part, way * 3 + piece).start()
    for piece in range(PIECES):
        for way in range(2):
            cot_forward(way, piece).wait_recv()
        cot_share(3, piece).start()
    for part in range(2):
        for way in range(2):
            dec_z(part, way, 3).wait_recv()
        dec_share(part, 6).start()

    acc[...] = jnp.zeros_like(acc)
    loads[0].wait()
    loads[1].wait()
    for which in range(3):
        loads[3 + which].wait()
    cot_sibling().wait_recv()
    hid_sibling().wait_recv()
    for which in range(4):
        for piece in range(PIECES):
            cot_share(which, piece).wait_recv()
    for part in range(2):
        for slot in range(8):
            dec_share(part, slot).wait_recv()

    def stage_sum(wave):
        for source in range(2):
            hid_half_wait(wave, source)

        def tile(index, carry):
            cols = pl.ds(aligned(index * PCOL, PCOL), PCOL)
            value = lax.dot_general(
                cotv[:, cols], hidv[:, wave_cols(wave)],
                (((0,), (0,)), ((), ())), preferred_element_type=jnp.float32,
            )
            pv[wave, cols, :] = value.astype(jnp.bfloat16)
            return carry

        lax.fori_loop(0, PIECES, tile, 0)
        for way in range(2):
            ring_first(wave, way).start()

    def stage_ring(wave, step):
        for way in range(2):
            pltpu.make_async_copy(
                rv.at[wave, way, step - 1], rv.at[wave, way, step - 1],
                r_recv.at[wave, way, step - 1],
            ).wait()
            own = pv[wave, ring_rows(ring_block(way, step)), way * LANE:(way + 1) * LANE]
            total = rv[wave, way, step - 1].astype(jnp.float32) + own.astype(jnp.float32)
            rv[wave, way, step - 1] = total.astype(jnp.bfloat16)
            ring_next(wave, way, step).start()

    def stage_home(wave):
        step = NZ - 1
        for way in range(2):
            pltpu.make_async_copy(
                rv.at[wave, way, step - 1], rv.at[wave, way, step - 1],
                r_recv.at[wave, way, step - 1],
            ).wait()
            lanes = slice(way * LANE, (way + 1) * LANE)
            own = pv[wave, ring_rows(z), lanes]
            total = rv[wave, way, step - 1].astype(jnp.float32) + own.astype(jnp.float32)
            pv[wave, ring_rows(z), lanes] = total.astype(jnp.bfloat16)
        grad_swap(wave).start()

    def adamw(wave, half, gradient):
        cols = state_cols(wave, half)
        master_now = st[0, :, cols]
        one = beta_one * st[1, :, cols] + (1.0 - beta_one) * gradient
        two = beta_two * st[2, :, cols] + (1.0 - beta_two) * gradient * gradient
        update = one / correct_one / (jnp.sqrt(two / correct_two) + epsilon)
        fresh = master_now - learn_rate * (update + decay_rate * master_now)
        st[0, :, cols] = fresh
        st[1, :, cols] = one
        st[2, :, cols] = two
        wv[grp, wave, :, pl.ds(aligned(half * WCOL, WCOL), WCOL)] = fresh.astype(jnp.bfloat16)

    def stage_update(wave):
        adamw(wave, core, pv[wave, chip_rows(core), :].astype(jnp.float32))
        grad_swap(wave).wait_recv()
        adamw(wave, other, gx[wave].astype(jnp.float32))
        weights_pair(wave).start()
        for way in range(2):
            weights_y(wave, 0, way).start()
        for half in range(2):
            for which in range(3):
                store_out(wave, half, which).start()

    def stage_spread(wave):
        weights_pair(wave).wait_recv()
        for way in range(2):
            weights_y(wave, 1, way).start()
        for way in range(2):
            weights_y(wave, 0, way).wait_recv()
            weights_forward(wave, 0, way).start()

    def stage_far(wave):
        for way in range(2):
            weights_y(wave, 1, way).wait_recv()
            weights_forward(wave, 1, way).start()

    def stage_decode(wave):
        for part in range(2):
            for way in range(2):
                weights_forward(wave, part, way).wait_recv()

        lanes = pl.ds(aligned(lax.rem(wave, 2) * WCOL, WCOL), WCOL)

        def bucket_step(index, total):
            first = held[index] * 4 + wave // 2
            for half in range(2):
                total = total + lax.dot_general(
                    xv[first + 2 * half, :, lanes],
                    wv[index, wave, :, half * WCOL:(half + 1) * WCOL],
                    (((1,), (1,)), ((), ())), preferred_element_type=jnp.float32,
                )
            return total

        acc[...] = lax.fori_loop(0, 8, bucket_step, acc[...])

    def tick(now, carry):
        def each(wave, inner):
            stage = now - LAG * wave
            pl.when(stage == 0)(lambda: stage_sum(wave))
            pl.when(jnp.logical_and(stage >= 1, stage <= 6))(
                lambda: stage_ring(wave, stage)
            )
            pl.when(stage == 7)(lambda: stage_home(wave))
            pl.when(stage == 8)(lambda: stage_update(wave))
            pl.when(stage == 9)(lambda: stage_spread(wave))
            pl.when(stage == 10)(lambda: stage_far(wave))
            pl.when(stage == LAST)(lambda: stage_decode(wave))
            return inner

        return lax.fori_loop(0, WAVES, each, carry)

    lax.fori_loop(0, LAST + 1 + LAG * (WAVES - 1), tick, 0)
    dec_out[...] = acc[...].astype(jnp.bfloat16)

    cot_sibling().wait_send()
    hid_sibling().wait_send()
    dec_half().wait_send()
    for piece in range(PIECES):
        cot_cross(piece).wait_send()
        for way in range(2):
            cot_y(way, piece).wait_send()
            cot_forward(way, piece).wait_send()
        for which in range(4):
            cot_share(which, piece).wait_send()
    for part in range(2):
        for way in range(2):
            for step in range(4):
                dec_z(part, way, step).wait_send()
        for slot in range(8):
            dec_share(part, slot).wait_send()

    def drain(wave, carry):
        for target in range(2):
            hid_half(wave, target).wait_send()
        for way in range(2):
            ring_first(wave, way).wait_send()
            for step in range(1, NZ - 1):
                ring_next(wave, way, step).wait_send()
        grad_swap(wave).wait_send()
        weights_pair(wave).wait_send()
        for part in range(2):
            for way in range(2):
                weights_y(wave, part, way).wait_send()
                weights_forward(wave, part, way).wait_send()
        for half in range(2):
            for which in range(3):
                store_out(wave, half, which).wait()
        return carry

    lax.fori_loop(0, WAVES, drain, 0)


def body(hidden_acts, cotangent, master, moment_one, moment_two, held_bucket, decode_in):
    any_spec = pl.BlockSpec(memory_space=pl.ANY)
    vmem = pltpu.VMEM
    sems = pltpu.SemaphoreType.DMA
    bf16, f32 = jnp.bfloat16, jnp.float32
    state = jax.ShapeDtypeStruct((OWN, BUCKET), f32)
    steps = NZ - 1
    pairs = [
        (2,), (PIECES,), (2, PIECES), (2, PIECES), (4, PIECES), (WAVES, 2), (1,),
        (2, 2, 4), (2, 8), (WAVES, 2, steps), (WAVES,), (WAVES,), (WAVES, 2, 2),
        (WAVES, 2, 2),
    ]
    both = [sems(shape) for shape in pairs for _ in range(2)]
    return pl.pallas_call(
        kernel,
        out_shape=(state, state, state, jax.ShapeDtypeStruct((ROWS, OWN), bf16)),
        in_specs=[any_spec] * 5 + [pl.BlockSpec(memory_space=pltpu.SMEM), any_spec],
        out_specs=(any_spec, any_spec, any_spec, pl.BlockSpec(memory_space=pltpu.VMEM)),
        scratch_shapes=[
            vmem((4 * TOK, HALF), bf16),
            vmem((4 * TOK, COLS), bf16),
            vmem((WAVES, HALF, WCOL), bf16),
            vmem((WAVES, 2, steps, CHIP, LANE), bf16),
            vmem((WAVES, OWN, WCOL), bf16),
            vmem((3, OWN, BUCKET), f32),
            vmem((8, WAVES, OWN, 2 * WCOL), bf16),
            vmem((32, ROWS, DCOL), bf16),
            vmem((ROWS, OWN), f32),
            sems((6,)),
            *both,
            sems((WAVES, 2, 3)),
        ],
        compiler_params=pltpu.CompilerParams(
            collective_id=0, has_side_effects=True, vmem_limit_bytes=58 * 2**20
        ),
        cost_estimate=pl.CostEstimate(
            flops=12_000_000_000, bytes_accessed=30_000_000, transcendentals=0
        ),
    )(hidden_acts, cotangent, master, moment_one, moment_two, held_bucket, decode_in)


def solution(mesh):
    placed = (
        P("shard", "grp"),
        P("shard", None),
        P("shard", "grp"),
        P("shard", "grp"),
        P("shard", "grp"),
        P(),
        P("grp", "shard"),
    )
    return jax.shard_map(
        body,
        mesh=mesh,
        in_specs=placed,
        out_specs=(P("shard", "grp"), P("shard", "grp"), P("shard", "grp"), P("grp", "shard")),
        check_vma=False,
    )
```

```python
import jax
import jax.numpy as jnp
from jax import lax
from jax.experimental import pallas as pl
from jax.experimental.pallas import tpu as pltpu
from jax.sharding import PartitionSpec as P

beta_one = 0.9
beta_two = 0.95
learn_rate = 0.001
decay_rate = 0.1
epsilon = 1e-08
correct_one = 1.0 - 0.9**50
correct_two = 1.0 - 0.95**50

NX, NY, NZ = 4, 4, 8
FEAT = 5120
HALF = FEAT // 2
OWN = 160
CHIP = 2 * OWN
TOK = 512
BUCKET = 2048
COLS = BUCKET // 2
WAVES = 4
WCOL = COLS // WAVES
LANE = WCOL // 2
PIECES = 4
PCOL = HALF // PIECES
PROW = TOK // NY
ROWS = 128
DCOL = 512
RINGS = WAVES + 1
LAST = 14
GROUPS = 8
HROWS = ROWS // 2
SLICES = 16


def aligned(value, step):
    return pl.multiple_of(value, step)


def device_at(x, y, z, core):
    x, y, z = lax.rem(x, NX), lax.rem(y, NY), lax.rem(z, NZ)
    return {
        "grp": lax.rem(x, 2) * NY + y,
        "shard": (x // 2) * 16 + z * 2 + core,
    }


def kernel(
    hid, cot, master, mom_one, mom_two, held, dec,
    master_out, one_out, two_out, dec_out,
    cotv, cotx, hidv, pv, rv, gx, hx, st, wv, a2, pick, xv, acc, dsend, drecv,
    local_sem, a_recv, in_send, in_recv,
    cc_send, cc_recv, cy_send, cy_recv, cf_send, cf_recv, cs_send, cs_recv,
    hx_send, hx_recv, xx_send, xx_recv, xz_send, xz_recv, xs_send, xs_recv,
    r_send, r_recv, g_send, g_recv, h_send, h_recv, a_send, p_send, p_recv, d_send, d_recv, out_sem,
):
    grp = lax.axis_index("grp")
    shard = lax.axis_index("shard")
    x_lo, y = grp // NY, lax.rem(grp, NY)
    x_hi, z, core = shard // 16, lax.rem(shard, 16) // 2, lax.rem(shard, 2)
    x = x_hi * 2 + x_lo
    other = 1 - core

    sibling = device_at(x, y, z, other)
    z_up, z_down = device_at(x, y, z + 1, core), device_at(x, y, z + NZ - 1, core)
    y_up, y_down = device_at(x, y + 1, z, core), device_at(x, y + NY - 1, z, core)
    x_half = device_at(x + 2, y, z, core)
    x_half_other = device_at(x + 2, y, z, other)
    x_cross = device_at(3 - x, y, z, core)
    slot_here = shard // 2
    z_way = (z_up, z_down)
    y_way = (y_up, y_down)

    def remote(src, dst, send, recv, device):
        return pltpu.make_async_remote_copy(
            src_ref=src, dst_ref=dst, send_sem=send, recv_sem=recv,
            device_id=device, device_id_type=pl.DeviceIdType.MESH,
        )

    barrier = pltpu.get_barrier_semaphore()
    partners = (
        sibling, z_up, z_down, y_up, y_down, x_half, x_half_other, x_cross,
    )

    def greet(device):
        pl.semaphore_signal(
            barrier, inc=1, device_id=device, device_id_type=pl.DeviceIdType.MESH
        )

    def peer(offset):
        return {"grp": lax.rem(grp + offset, GROUPS), "shard": shard}

    for partner in partners:
        greet(partner)
    for offset in range(1, GROUPS):
        greet(peer(offset))
    for bucket in range(GROUPS):
        source = bucket * 4 + shard // 8

        @pl.when(source != shard)
        def _():
            greet({"grp": grp, "shard": source})

    keeps_one = jnp.where(lax.rem(shard, 4) == shard // 8, 1, 0)

    mine = pl.ds(aligned(core * TOK, TOK), TOK)
    loads = [
        pltpu.make_async_copy(
            cot.at[:, pl.ds(aligned(x_hi * HALF, HALF), HALF)], cotv.at[mine, :],
            local_sem.at[0],
        ),
        pltpu.make_async_copy(
            hid.at[:, pl.ds(aligned(core * COLS, COLS), COLS)], hidv.at[mine, :],
            local_sem.at[1],
        ),
        pltpu.make_async_copy(master, st.at[0], local_sem.at[2]),
        pltpu.make_async_copy(mom_one, st.at[1], local_sem.at[3]),
        pltpu.make_async_copy(mom_two, st.at[2], local_sem.at[4]),
        pltpu.make_async_copy(
            cot.at[:, pl.ds(aligned((1 - x_hi) * HALF, HALF), HALF)], cotx.at[mine, :],
            local_sem.at[5],
        ),
    ]
    for copy in loads:
        copy.start()

    def cot_sibling():
        return remote(
            cot.at[:, pl.ds(aligned(x_hi * HALF, HALF), HALF)], cotv.at[mine, :],
            in_send.at[0], in_recv.at[0], sibling,
        )

    def cotx_sibling():
        return remote(
            cot.at[:, pl.ds(aligned((1 - x_hi) * HALF, HALF), HALF)], cotx.at[mine, :],
            in_send.at[2], in_recv.at[2], sibling,
        )

    def hid_sibling():
        return remote(
            hid.at[:, pl.ds(aligned(other * COLS, COLS), COLS)], hidv.at[mine, :],
            in_send.at[1], in_recv.at[1], sibling,
        )

    def cot_rows(owner, first, count):
        return pl.ds(aligned((2 + core) * TOK + owner * PROW + first, 64), count)

    def cot_cols(piece):
        return pl.ds(aligned(piece * PCOL, PCOL), PCOL)

    def cot_cross(piece):
        return remote(
            cot.at[
                pl.ds(aligned(y * PROW, PROW), PROW),
                pl.ds(aligned((1 - x_hi) * HALF + piece * PCOL, 128), PCOL),
            ],
            cotv.at[cot_rows(y, 0, PROW), cot_cols(piece)],
            cc_send.at[piece], cc_recv.at[piece], x_cross,
        )

    def cot_y(way, piece):
        part = cotv.at[cot_rows(y, 0, PROW), cot_cols(piece)]
        return remote(
            part, part, cy_send.at[way, piece], cy_recv.at[way, piece], y_way[way]
        )

    def cot_forward(way, piece):
        owner = lax.rem(y + (NY - 1 if way == 0 else 1), NY)
        part = cotv.at[cot_rows(owner, way * (PROW // 2), PROW // 2), cot_cols(piece)]
        return remote(
            part, part, cf_send.at[way, piece], cf_recv.at[way, piece], y_way[way]
        )

    def cot_share(which, piece):
        owner = lax.rem(y + (0, NY - 1, 1, 2)[which], NY)
        part = cotv.at[cot_rows(owner, 0, PROW), cot_cols(piece)]
        return remote(
            part, part, cs_send.at[which, piece], cs_recv.at[which, piece], sibling
        )

    def wave_cols(wave):
        return pl.ds(aligned(wave * WCOL, WCOL), WCOL)

    def hid_half(wave, target):
        rows = pl.ds(aligned((2 + core) * TOK, TOK), TOK)
        device = device_at(x + 2, y, z, target)
        return remote(
            hid.at[:, pl.ds(aligned(target * COLS + wave * WCOL, WCOL), WCOL)],
            hidv.at[rows, wave_cols(wave)],
            hx_send.at[wave, target], hx_recv.at[wave, core], device,
        )

    def hid_half_wait(wave, source):
        part = hidv.at[pl.ds((2 + source) * TOK, TOK), wave_cols(wave)]
        pltpu.make_async_copy(part, part, hx_recv.at[wave, source]).wait()

    def dec_target(index, which):
        return (lax.rem(shard, 4) * 4 + index) * 2 + which

    def dec_slice(index, which):
        return dec.at[pl.ds(which * HROWS, HROWS), pl.ds(index * 128, 128)]

    def dec_away(index, which):
        return remote(
            dec_slice(index, which), a2.at[shard // 4],
            a_send.at[index, which], a_recv.at[shard // 4],
            {"grp": grp, "shard": dec_target(index, which)},
        )

    def dec_here(index, which):
        return pltpu.make_async_copy(
            dec_slice(index, which), a2.at[shard // 4], a_recv.at[shard // 4]
        )

    def dec_pick(offset):
        return remote(
            pick.at[lax.rem(grp + offset, GROUPS)], xv.at[slot_here, core, grp],
            p_send.at[offset], p_recv.at[offset], peer(offset),
        )

    def dec_index(half, place):
        return half * 8 + place

    def dec_half():
        block = xv.at[slot_here, core]
        return remote(block, block, xx_send.at[0], xx_recv.at[0], x_half)

    def dec_z(part, way, step):
        half = x_hi if part == 0 else 1 - x_hi
        place = lax.rem(z + (NZ - step if way == 0 else step), NZ)
        groups = pl.ds(0, GROUPS)
        if step == 3:
            groups = pl.ds(way * (GROUPS // 2), GROUPS // 2)
        block = xv.at[dec_index(half, place), core, groups]
        return remote(
            block, block, xz_send.at[part, way, step], xz_recv.at[part, way, step],
            z_way[way],
        )

    def dec_share(part, slot):
        half = x_hi if part == 0 else 1 - x_hi
        shift = (NZ - 1, NZ - 2, NZ - 3, 1, 2, 3, 4, 0)[slot]
        block = xv.at[dec_index(half, lax.rem(z + shift, NZ)), core]
        return remote(
            block, block, xs_send.at[part, slot], xs_recv.at[part, slot], sibling
        )

    def partial_out(offset):
        return remote(
            dsend.at[lax.rem(grp + offset, GROUPS)], drecv.at[offset],
            d_send.at[offset], d_recv.at[offset], peer(offset),
        )

    def ring_block(way, step):
        if way == 0:
            return lax.rem(z + 4 - step, NZ)
        return lax.rem(z + 4 + step, NZ)

    def ring_rows(place):
        return pl.ds(aligned(place * CHIP, CHIP), CHIP)

    def ring_own(wave, way, part, step):
        return remote(
            pv.at[wave, ring_rows(ring_block(way, step)), pl.ds(part * LANE, LANE)],
            rv.at[wave, way, part, step],
            r_send.at[wave, way, part, step], r_recv.at[wave, way, part, step],
            z_way[way],
        )

    def ring_next(wave, way, part, step):
        return remote(
            rv.at[wave, way, part, step - 1], rv.at[wave, way, part, step],
            r_send.at[wave, way, part, step], r_recv.at[wave, way, part, step],
            z_way[way],
        )

    def ring_wait(wave, way, part, step):
        block = rv.at[wave, way, part, step]
        pltpu.make_async_copy(block, block, r_recv.at[wave, way, part, step]).wait()

    def chip_rows(which):
        return pl.ds(aligned(z * CHIP + which * OWN, 32), OWN)

    def grad_swap(wave):
        return remote(
            pv.at[wave, chip_rows(other), :], gx.at[wave],
            g_send.at[wave], g_recv.at[wave], sibling,
        )

    def home_half():
        return remote(
            pv.at[0, ring_rows(z), :], hx, h_send.at[0], h_recv.at[0], x_half
        )

    def state_cols(wave, half):
        return pl.ds(aligned(half * COLS + wave * WCOL, WCOL), WCOL)

    def store_out(wave, half, which):
        cols = state_cols(wave, half)
        target = (master_out, one_out, two_out)[which]
        return pltpu.make_async_copy(
            st.at[which, :, cols], target.at[:, cols], out_sem.at[wave, half, which]
        )

    pl.semaphore_wait(barrier, len(partners) + GROUPS - 1 + GROUPS - keeps_one)
    for piece in range(PIECES):
        cot_cross(piece).start()
    for index in range(4):
        for which in range(2):
            stays = dec_target(index, which) == shard
            pl.when(jnp.logical_not(stays))(lambda: dec_away(index, which).start())
            pl.when(stays)(lambda: dec_here(index, which).start())
    hid_sibling().start()
    cotx_sibling().start()
    cot_sibling().start()

    def dec_begin():
        for bucket in range(GROUPS):
            part = a2.at[bucket]
            pltpu.make_async_copy(part, part, a_recv.at[bucket]).wait()
        for offset in range(1, GROUPS):
            target = lax.rem(grp + offset, GROUPS)
            pick[target] = a2[held[target]]
            dec_pick(offset).start()
        xv[slot_here, core, grp] = a2[held[grp]]

    def dec_own():
        for offset in range(1, GROUPS):
            dec_pick(offset).wait_recv()
        dec_half().start()
        for way in range(2):
            dec_z(0, way, 0).start()
        dec_share(0, 7).start()

    def dec_first():
        dec_half().wait_recv()
        for way in range(2):
            dec_z(1, way, 0).start()
        dec_share(1, 7).start()

    def dec_step(step):
        for part in range(2):
            for way in range(2):
                dec_z(part, way, step).wait_recv()
                dec_z(part, way, step + 1).start()
                dec_share(part, way * 3 + step).start()

    def dec_last():
        for part in range(2):
            for way in range(2):
                dec_z(part, way, 3).wait_recv()
            dec_share(part, 6).start()

    def cot_near(piece):
        for way in range(2):
            cot_y(way, piece).wait_recv()
            cot_forward(way, piece).start()
            cot_share(1 + way, piece).start()

    def cot_far(piece):
        for way in range(2):
            cot_forward(way, piece).wait_recv()
        cot_share(3, piece).start()

    def cot_begin(piece):
        cot_cross(piece).wait_recv()
        for way in range(2):
            cot_y(way, piece).start()
        cot_share(0, piece).start()

    def hid_begin(wave):
        for target in range(2):
            hid_half(wave, target).start()

    acc[...] = jnp.zeros_like(acc)
    cot_begin(0)
    loads[1].wait()
    loads[5].wait()
    hid_sibling().wait_recv()
    cotx_sibling().wait_recv()

    def multiply(ring, rows, left, cols):
        def tile(index, carry):
            part = pl.ds(aligned(index * PCOL, PCOL), PCOL)
            value = lax.dot_general(
                left[rows, part], hidv[rows, cols],
                (((0,), (0,)), ((), ())), preferred_element_type=jnp.float32,
            )
            pv[ring, part, :] = value.astype(jnp.bfloat16)
            return carry

        lax.fori_loop(0, PIECES, tile, 0)
        for way in range(2):
            ring_own(ring, way, way, 0).start()
        for way in range(2):
            ring_own(ring, way, 1 - way, 1).start()

    def stage_sum(ring):
        pl.when(ring == 0)(
            lambda: multiply(0, slice(0, 2 * TOK), cotx, slice(0, WCOL))
        )

        @pl.when(ring == 1)
        def _():
            loads[0].wait()
            cot_sibling().wait_recv()
            multiply(1, slice(0, 2 * TOK), cotv, slice(0, WCOL))

        @pl.when(ring > 1)
        def _():
            for source in range(2):
                hid_half_wait(ring - 1, source)
            multiply(ring, slice(0, 4 * TOK), cotv, wave_cols(ring - 1))

    def ring_add(wave, way, part, step):
        ring_wait(wave, way, part, step - 1)
        own = pv[wave, ring_rows(ring_block(way, step)), part * LANE:(part + 1) * LANE]
        total = rv[wave, way, part, step - 1].astype(jnp.float32) + own.astype(jnp.float32)
        rv[wave, way, part, step - 1] = total.astype(jnp.bfloat16)
        ring_next(wave, way, part, step).start()

    def stage_near(wave):
        for way in range(2):
            ring_add(wave, way, way, 1)

    def stage_ring(wave, step):
        for part in range(2):
            for way in range(2):
                ring_add(wave, way, part, step)

    def home_sum(ring):
        for part in range(2):
            for way in range(2):
                ring_wait(ring, way, part, 3)
            lanes = slice(part * LANE, (part + 1) * LANE)
            total = pv[ring, ring_rows(z), lanes].astype(jnp.float32)
            for way in range(2):
                total = total + rv[ring, way, part, 3].astype(jnp.float32)
            pv[ring, ring_rows(z), lanes] = total.astype(jnp.bfloat16)

    def stage_home(ring):
        home_sum(ring)
        pl.when(ring == 0)(lambda: home_half().start())

        @pl.when(ring == 1)
        def _():
            home_half().wait_recv()
            total = pv[1, ring_rows(z), :].astype(jnp.float32) + hx[...].astype(jnp.float32)
            pv[1, ring_rows(z), :] = total.astype(jnp.bfloat16)

        pl.when(ring > 0)(lambda: grad_swap(ring).start())

    def adamw(wave, half, gradient):
        cols = state_cols(wave, half)
        master_now = st[0, :, cols]
        one = beta_one * st[1, :, cols] + (1.0 - beta_one) * gradient
        two = beta_two * st[2, :, cols] + (1.0 - beta_two) * gradient * gradient
        update = one / correct_one / (jnp.sqrt(two / correct_two) + epsilon)
        fresh = master_now - learn_rate * (update + decay_rate * master_now)
        st[0, :, cols] = fresh
        st[1, :, cols] = one
        st[2, :, cols] = two
        for which in range(3):
            store_out(wave, half, which).start()
        wv[half, :, wave_cols(wave)] = fresh.astype(jnp.bfloat16)

    def decode(wave):
        for half in range(2):
            first = half * (SLICES // 2) + 2 * wave
            for which in range(2):
                inputs = jnp.concatenate(
                    [
                        xv[first + part, which].reshape(GROUPS * HROWS, 128)
                        for part in range(2)
                    ],
                    axis=1,
                )
                acc[which] += lax.dot_general(
                    inputs, wv[half, :, wave_cols(wave)], (((1,), (1,)), ((), ())),
                    preferred_element_type=jnp.float32,
                )

    def stage_update(ring):
        wave = ring - 1
        adamw(wave, core, pv[ring, chip_rows(core), :].astype(jnp.float32))
        grad_swap(ring).wait_recv()
        adamw(wave, other, gx[ring].astype(jnp.float32))
        pl.when(ring > 1)(lambda: decode(wave))

    def tick(now, carry):
        @pl.when(now == 0)
        def _():
            cot_begin(1)
            dec_begin()

        @pl.when(now == 1)
        def _():
            cot_begin(2)
            cot_begin(3)
            dec_own()

        @pl.when(now == 2)
        def _():
            cot_near(0)
            cot_near(1)
            dec_first()

        @pl.when(now == 3)
        def _():
            cot_far(0)
            cot_near(2)
            hid_begin(1)
            cot_near(3)
            cot_far(1)

        @pl.when(now == 4)
        def _():
            cot_far(2)
            cot_far(3)
            hid_begin(2)
            dec_step(0)

        @pl.when(now == 5)
        def _():
            hid_begin(3)
            for which in range(3):
                loads[2 + which].wait()
            for which in range(4):
                for piece in range(PIECES):
                    cot_share(which, piece).wait_recv()

        pl.when(now == 6)(lambda: dec_step(1))
        pl.when(now == 8)(lambda: dec_step(2))
        pl.when(now == 9)(dec_last)

        @pl.when(now == 10)
        def _():
            for part in range(2):
                for slot in range(8):
                    dec_share(part, slot).wait_recv()
            decode(0)

        def each(ring, inner):
            stage = now - jnp.where(ring < 2, ring, 2 * ring + 1)
            home = jnp.where(ring == 1, 6, 4)
            pl.when(stage == 0)(lambda: stage_sum(ring))
            pl.when(stage == 1)(lambda: stage_near(ring))
            pl.when(jnp.logical_or(stage == 2, stage == 3))(
                lambda: stage_ring(ring, stage)
            )
            pl.when(stage == home)(lambda: stage_home(ring))
            pl.when(jnp.logical_and(stage == home + 1, ring > 0))(
                lambda: stage_update(ring)
            )
            return inner

        return lax.fori_loop(0, RINGS, each, carry)

    lax.fori_loop(0, LAST + 1, tick, 0)

    def own_rows(group):
        rows = pl.ds(aligned(group * HROWS, HROWS), HROWS)
        return acc[0, rows, :], acc[1, rows, :]

    for offset in range(1, GROUPS):
        group = lax.rem(grp + offset, GROUPS)
        dsend[group] = jnp.concatenate(own_rows(group), axis=0).T.astype(jnp.bfloat16)
        partial_out(offset).start()
    total = jnp.concatenate(own_rows(grp), axis=0).T
    for offset in range(1, GROUPS):
        partial_out(offset).wait_recv()
        total = total + drecv[offset].astype(jnp.float32)
    dec_out[...] = total.astype(jnp.bfloat16)

    cot_sibling().wait_send()
    cotx_sibling().wait_send()
    home_half().wait_send()
    hid_sibling().wait_send()
    dec_half().wait_send()
    for index in range(4):
        for which in range(2):
            stays = dec_target(index, which) == shard
            pl.when(jnp.logical_not(stays))(lambda: dec_away(index, which).wait_send())
    for offset in range(1, GROUPS):
        dec_pick(offset).wait_send()
        partial_out(offset).wait_send()
    for piece in range(PIECES):
        cot_cross(piece).wait_send()
        for way in range(2):
            cot_y(way, piece).wait_send()
            cot_forward(way, piece).wait_send()
        for which in range(4):
            cot_share(which, piece).wait_send()
    for part in range(2):
        for way in range(2):
            for step in range(4):
                dec_z(part, way, step).wait_send()
        for slot in range(8):
            dec_share(part, slot).wait_send()

    def drain(ring, carry):
        for way in range(2):
            for part in range(2):
                for step in range(0 if way == part else 1, 4):
                    ring_own(ring, way, part, step).wait_send()

        @pl.when(ring > 0)
        def _():
            grad_swap(ring).wait_send()
            for half in range(2):
                for which in range(3):
                    store_out(ring - 1, half, which).wait()

        @pl.when(ring > 1)
        def _():
            for target in range(2):
                hid_half(ring - 1, target).wait_send()

        return carry

    lax.fori_loop(0, RINGS, drain, 0)


def body(hidden_acts, cotangent, master, moment_one, moment_two, held_bucket, decode_in):
    any_spec = pl.BlockSpec(memory_space=pl.ANY)
    vmem = pltpu.VMEM
    sems = pltpu.SemaphoreType.DMA
    bf16, f32 = jnp.bfloat16, jnp.float32
    state = jax.ShapeDtypeStruct((OWN, BUCKET), f32)
    pairs = [
        (3,), (PIECES,), (2, PIECES), (2, PIECES), (4, PIECES), (WAVES, 2), (1,),
        (2, 2, 4), (2, 8), (RINGS, 2, 2, 4), (RINGS,), (1,),
    ]
    both = [sems(shape) for shape in pairs for _ in range(2)]
    *states, decoded = pl.pallas_call(
        kernel,
        out_shape=(state, state, state, jax.ShapeDtypeStruct((OWN, ROWS), bf16)),
        in_specs=[any_spec] * 5 + [pl.BlockSpec(memory_space=pltpu.SMEM), any_spec],
        out_specs=(any_spec, any_spec, any_spec, pl.BlockSpec(memory_space=pltpu.VMEM)),
        scratch_shapes=[
            vmem((4 * TOK, HALF), bf16),
            vmem((2 * TOK, HALF), bf16),
            vmem((4 * TOK, COLS), bf16),
            vmem((RINGS, HALF, WCOL), bf16),
            vmem((RINGS, 2, 2, 4, CHIP, LANE), bf16),
            vmem((RINGS, OWN, WCOL), bf16),
            vmem((CHIP, WCOL), bf16),
            vmem((3, OWN, BUCKET), f32),
            vmem((2, OWN, COLS), bf16),
            vmem((GROUPS, HROWS, 128), bf16),
            vmem((GROUPS, HROWS, 128), bf16),
            vmem((SLICES, 2, GROUPS, HROWS, 128), bf16),
            vmem((2, GROUPS * HROWS, OWN), f32),
            vmem((GROUPS, OWN, ROWS), bf16),
            vmem((GROUPS, OWN, ROWS), bf16),
            sems((6,)),
            sems((GROUPS,)),
            *both,
            sems((4, 2)),
            *[sems((GROUPS,)) for _ in range(4)],
            sems((WAVES, 2, 3)),
        ],
        compiler_params=pltpu.CompilerParams(
            collective_id=0, has_side_effects=True, vmem_limit_bytes=58 * 2**20
        ),
        cost_estimate=pl.CostEstimate(
            flops=12_000_000_000, bytes_accessed=30_000_000, transcendentals=0
        ),
    )(hidden_acts, cotangent, master, moment_one, moment_two, held_bucket, decode_in)
    return (*states, decoded.T)


def solution(mesh):
    placed = (
        P("shard", "grp"),
        P("shard", None),
        P("shard", "grp"),
        P("shard", "grp"),
        P("shard", "grp"),
        P(),
        P("grp", "shard"),
    )
    return jax.shard_map(
        body,
        mesh=mesh,
        in_specs=placed,
        out_specs=(P("shard", "grp"), P("shard", "grp"), P("shard", "grp"), P("grp", "shard")),
        check_vma=False,
    )
```

```python
import jax
import jax.numpy as jnp
from jax import lax
from jax.experimental import pallas as pl
from jax.experimental.pallas import tpu as pltpu
from jax.sharding import PartitionSpec as P

beta_one = 0.9
beta_two = 0.95
learn_rate = 0.001
decay_rate = 0.1
epsilon = 1e-08
correct_one = 1.0 - 0.9**50
correct_two = 1.0 - 0.95**50

NX, NY, NZ = 4, 4, 8
FEAT = 5120
HALF = FEAT // 2
OWN = 160
CHIP = 2 * OWN
TOK = 512
BUCKET = 2048
COLS = BUCKET // 2
WAVES = 4
WCOL = COLS // WAVES
LANE = WCOL // 2
PIECES = 4
PCOL = HALF // PIECES
PROW = TOK // NY
ROWS = 128
DCOL = 512
RINGS = WAVES + 1
START = (0, 1, 3, 4, 5)
LAST = START[-1] + 5
GROUPS = 8
HROWS = ROWS // 2
SLICES = 16


def aligned(value, step):
    return pl.multiple_of(value, step)


def device_at(x, y, z, core):
    x, y, z = lax.rem(x, NX), lax.rem(y, NY), lax.rem(z, NZ)
    return {
        "grp": lax.rem(x, 2) * NY + y,
        "shard": (x // 2) * 16 + z * 2 + core,
    }


def kernel(
    hid, cot, master, mom_one, mom_two, held, dec,
    master_out, one_out, two_out, dec_out,
    cotv, cotx, hidv, pv, rv, gx, hx, wv, a2, pick, xv, acc, dsend, drecv,
    local_sem, a_recv, in_send, in_recv,
    cc_send, cc_recv, cy_send, cy_recv, cf_send, cf_recv, cs_send, cs_recv,
    hx_send, hx_recv, xx_send, xx_recv, xz_send, xz_recv, xs_send, xs_recv,
    r_send, r_recv, g_send, g_recv, h_send, h_recv, a_send, p_send, p_recv, d_send, d_recv,
):
    grp = lax.axis_index("grp")
    shard = lax.axis_index("shard")
    x_lo, y = grp // NY, lax.rem(grp, NY)
    x_hi, z, core = shard // 16, lax.rem(shard, 16) // 2, lax.rem(shard, 2)
    x = x_hi * 2 + x_lo
    other = 1 - core

    sibling = device_at(x, y, z, other)
    z_up, z_down = device_at(x, y, z + 1, core), device_at(x, y, z + NZ - 1, core)
    y_up, y_down = device_at(x, y + 1, z, core), device_at(x, y + NY - 1, z, core)
    x_half = device_at(x + 2, y, z, core)
    x_half_other = device_at(x + 2, y, z, other)
    x_cross = device_at(3 - x, y, z, core)
    slot_here = shard // 2
    z_way = (z_up, z_down)
    y_way = (y_up, y_down)

    def remote(src, dst, send, recv, device):
        return pltpu.make_async_remote_copy(
            src_ref=src, dst_ref=dst, send_sem=send, recv_sem=recv,
            device_id=device, device_id_type=pl.DeviceIdType.MESH,
        )

    barrier = pltpu.get_barrier_semaphore()
    partners = (
        sibling, z_up, z_down, y_up, y_down, x_half, x_half_other, x_cross,
    )

    def greet(device):
        pl.semaphore_signal(
            barrier, inc=1, device_id=device, device_id_type=pl.DeviceIdType.MESH
        )

    def peer(offset):
        return {"grp": lax.rem(grp + offset, GROUPS), "shard": shard}

    for partner in partners:
        greet(partner)
    for offset in range(1, GROUPS):
        greet(peer(offset))
    for bucket in range(GROUPS):
        source = bucket * 4 + shard // 8

        @pl.when(source != shard)
        def _():
            greet({"grp": grp, "shard": source})

    keeps_one = jnp.where(lax.rem(shard, 4) == shard // 8, 1, 0)

    mine = pl.ds(aligned(core * TOK, TOK), TOK)
    loads = [
        pltpu.make_async_copy(
            cot.at[:, pl.ds(aligned(x_hi * HALF, HALF), HALF)], cotv.at[mine, :],
            local_sem.at[0],
        ),
        pltpu.make_async_copy(
            hid.at[:, pl.ds(aligned(core * COLS, COLS), COLS)], hidv.at[mine, :],
            local_sem.at[1],
        ),
        pltpu.make_async_copy(master, master_out, local_sem.at[2]),
        pltpu.make_async_copy(mom_one, one_out, local_sem.at[3]),
        pltpu.make_async_copy(mom_two, two_out, local_sem.at[4]),
        pltpu.make_async_copy(
            cot.at[:, pl.ds(aligned((1 - x_hi) * HALF, HALF), HALF)], cotx.at[mine, :],
            local_sem.at[5],
        ),
    ]
    for copy in loads:
        copy.start()

    def cot_sibling():
        return remote(
            cot.at[:, pl.ds(aligned(x_hi * HALF, HALF), HALF)], cotv.at[mine, :],
            in_send.at[0], in_recv.at[0], sibling,
        )

    def cotx_sibling():
        return remote(
            cot.at[:, pl.ds(aligned((1 - x_hi) * HALF, HALF), HALF)], cotx.at[mine, :],
            in_send.at[2], in_recv.at[2], sibling,
        )

    def hid_sibling():
        return remote(
            hid.at[:, pl.ds(aligned(other * COLS, COLS), COLS)], hidv.at[mine, :],
            in_send.at[1], in_recv.at[1], sibling,
        )

    def cot_rows(owner, first, count):
        return pl.ds(aligned((2 + core) * TOK + owner * PROW + first, 64), count)

    def cot_cols(piece):
        return pl.ds(aligned(piece * PCOL, PCOL), PCOL)

    def cot_cross(piece):
        return remote(
            cot.at[
                pl.ds(aligned(y * PROW, PROW), PROW),
                pl.ds(aligned((1 - x_hi) * HALF + piece * PCOL, 128), PCOL),
            ],
            cotv.at[cot_rows(y, 0, PROW), cot_cols(piece)],
            cc_send.at[piece], cc_recv.at[piece], x_cross,
        )

    def cot_y(way, piece):
        part = cotv.at[cot_rows(y, 0, PROW), cot_cols(piece)]
        return remote(
            part, part, cy_send.at[way, piece], cy_recv.at[way, piece], y_way[way]
        )

    def cot_forward(way, piece):
        owner = lax.rem(y + (NY - 1 if way == 0 else 1), NY)
        part = cotv.at[cot_rows(owner, way * (PROW // 2), PROW // 2), cot_cols(piece)]
        return remote(
            part, part, cf_send.at[way, piece], cf_recv.at[way, piece], y_way[way]
        )

    def cot_share(which, piece):
        owner = lax.rem(y + (0, NY - 1, 1, 2)[which], NY)
        part = cotv.at[cot_rows(owner, 0, PROW), cot_cols(piece)]
        return remote(
            part, part, cs_send.at[which, piece], cs_recv.at[which, piece], sibling
        )

    def wave_cols(wave):
        return pl.ds(aligned(wave * WCOL, WCOL), WCOL)

    def hid_half(wave, target):
        rows = pl.ds(aligned((2 + core) * TOK, TOK), TOK)
        device = device_at(x + 2, y, z, target)
        return remote(
            hid.at[:, pl.ds(aligned(target * COLS + wave * WCOL, WCOL), WCOL)],
            hidv.at[rows, wave_cols(wave)],
            hx_send.at[wave, target], hx_recv.at[wave, core], device,
        )

    def hid_half_wait(wave, source):
        part = hidv.at[pl.ds((2 + source) * TOK, TOK), wave_cols(wave)]
        pltpu.make_async_copy(part, part, hx_recv.at[wave, source]).wait()

    def dec_target(index, which):
        return (lax.rem(shard, 4) * 4 + index) * 2 + which

    def dec_slice(index, which):
        return dec.at[pl.ds(which * HROWS, HROWS), pl.ds(index * 128, 128)]

    def dec_away(index, which):
        return remote(
            dec_slice(index, which), a2.at[shard // 4],
            a_send.at[index, which], a_recv.at[shard // 4],
            {"grp": grp, "shard": dec_target(index, which)},
        )

    def dec_here(index, which):
        return pltpu.make_async_copy(
            dec_slice(index, which), a2.at[shard // 4], a_recv.at[shard // 4]
        )

    def dec_pick(offset):
        return remote(
            pick.at[lax.rem(grp + offset, GROUPS)], xv.at[slot_here, core, grp],
            p_send.at[offset], p_recv.at[offset], peer(offset),
        )

    def dec_index(half, place):
        return half * 8 + place

    def dec_place(slot):
        shift = (NZ - 1, NZ - 2, NZ - 3, 1, 2, 3, 4, 0)[slot]
        return lax.rem(z + shift, NZ)

    def dec_half(slot):
        block = xv.at[dec_index(x_hi, dec_place(slot)), core]
        return remote(block, block, xx_send.at[slot], xx_recv.at[slot], x_half)

    def dec_z(way, step):
        place = lax.rem(z + (NZ - step if way == 0 else step), NZ)
        groups = pl.ds(0, GROUPS)
        if step == 3:
            groups = pl.ds(way * (GROUPS // 2), GROUPS // 2)
        block = xv.at[dec_index(x_hi, place), core, groups]
        return remote(
            block, block, xz_send.at[way, step], xz_recv.at[way, step], z_way[way]
        )

    def dec_share(part, slot):
        half = x_hi if part == 0 else 1 - x_hi
        block = xv.at[dec_index(half, dec_place(slot)), core]
        return remote(
            block, block, xs_send.at[part, slot], xs_recv.at[part, slot], sibling
        )

    def partial_out(offset):
        return remote(
            dsend.at[lax.rem(grp + offset, GROUPS)], drecv.at[offset],
            d_send.at[offset], d_recv.at[offset], peer(offset),
        )

    def ring_block(way, step):
        if way == 0:
            return lax.rem(z + 4 - step, NZ)
        return lax.rem(z + 4 + step, NZ)

    def ring_rows(place):
        return pl.ds(aligned(place * CHIP, CHIP), CHIP)

    def ring_own(wave, way, part, step):
        return remote(
            pv.at[wave, ring_rows(ring_block(way, step)), pl.ds(part * LANE, LANE)],
            rv.at[wave, way, part, step],
            r_send.at[wave, way, part, step], r_recv.at[wave, way, part, step],
            z_way[way],
        )

    def ring_next(wave, way, part, step):
        return remote(
            rv.at[wave, way, part, step - 1], rv.at[wave, way, part, step],
            r_send.at[wave, way, part, step], r_recv.at[wave, way, part, step],
            z_way[way],
        )

    def ring_wait(wave, way, part, step):
        block = rv.at[wave, way, part, step]
        pltpu.make_async_copy(block, block, r_recv.at[wave, way, part, step]).wait()

    def chip_rows(which):
        return pl.ds(aligned(z * CHIP + which * OWN, 32), OWN)

    def grad_swap(wave):
        return remote(
            pv.at[wave, chip_rows(other), :], gx.at[wave],
            g_send.at[wave], g_recv.at[wave], sibling,
        )

    def home_half():
        return remote(
            pv.at[0, ring_rows(z), :], hx, h_send.at[0], h_recv.at[0], x_half
        )

    def state_cols(wave, half):
        return pl.ds(aligned(half * COLS + wave * WCOL, WCOL), WCOL)

    pl.semaphore_wait(barrier, len(partners) + GROUPS - 1 + GROUPS - keeps_one)
    for piece in range(PIECES):
        cot_cross(piece).start()
    for index in range(4):
        for which in range(2):
            stays = dec_target(index, which) == shard
            pl.when(jnp.logical_not(stays))(lambda: dec_away(index, which).start())
            pl.when(stays)(lambda: dec_here(index, which).start())
    hid_sibling().start()
    cotx_sibling().start()
    cot_sibling().start()

    def dec_begin():
        for bucket in range(GROUPS):
            part = a2.at[bucket]
            pltpu.make_async_copy(part, part, a_recv.at[bucket]).wait()
        for offset in range(1, GROUPS):
            target = lax.rem(grp + offset, GROUPS)
            pick[target] = a2[held[target]]
            dec_pick(offset).start()
        xv[slot_here, core, grp] = a2[held[grp]]

    def dec_own():
        for offset in range(1, GROUPS):
            dec_pick(offset).wait_recv()
        for way in range(2):
            dec_z(way, 0).start()
        dec_half(7).start()
        dec_share(0, 7).start()

    def dec_step(step):
        for way in range(2):
            dec_z(way, step).wait_recv()
            dec_z(way, step + 1).start()
            dec_half(way * 3 + step).start()
            dec_share(0, way * 3 + step).start()

    def dec_last():
        for way in range(2):
            dec_z(way, 3).wait_recv()
        dec_half(6).start()
        dec_share(0, 6).start()

    def dec_cross(*slots):
        for slot in slots:
            dec_half(slot).wait_recv()
            dec_share(1, slot).start()

    def cot_near(piece):
        for way in range(2):
            cot_y(way, piece).wait_recv()
            cot_forward(way, piece).start()
            cot_share(1 + way, piece).start()

    def cot_far(piece):
        for way in range(2):
            cot_forward(way, piece).wait_recv()
        cot_share(3, piece).start()

    def cot_begin(piece):
        cot_cross(piece).wait_recv()
        for way in range(2):
            cot_y(way, piece).start()
        cot_share(0, piece).start()

    def cot_end():
        for which in range(4):
            for piece in range(PIECES):
                cot_share(which, piece).wait_recv()

    def state_end():
        for which in range(3):
            loads[2 + which].wait()

    def dec_end():
        for part in range(2):
            for slot in range(8):
                dec_share(part, slot).wait_recv()

    def hid_begin(wave):
        for target in range(2):
            hid_half(wave, target).start()

    acc[...] = jnp.zeros_like(acc)
    cot_begin(0)
    cot_begin(1)
    loads[1].wait()
    loads[5].wait()
    hid_sibling().wait_recv()
    cotx_sibling().wait_recv()

    def multiply(ring, rows, left, cols):
        def tile(index, carry):
            part = pl.ds(aligned(index * PCOL, PCOL), PCOL)
            value = lax.dot_general(
                left[rows, part], hidv[rows, cols],
                (((0,), (0,)), ((), ())), preferred_element_type=jnp.float32,
            )
            pv[ring, part, :] = value.astype(jnp.bfloat16)
            return carry

        lax.fori_loop(0, PIECES, tile, 0)
        for way in range(2):
            ring_own(ring, way, way, 0).start()
        for way in range(2):
            ring_own(ring, way, 1 - way, 1).start()

    def stage_sum(ring):
        pl.when(ring == 0)(
            lambda: multiply(0, slice(0, 2 * TOK), cotx, slice(0, WCOL))
        )

        @pl.when(ring == 1)
        def _():
            loads[0].wait()
            cot_sibling().wait_recv()
            multiply(1, slice(0, 2 * TOK), cotv, slice(0, WCOL))

        @pl.when(ring > 1)
        def _():
            for source in range(2):
                hid_half_wait(ring - 1, source)
            multiply(ring, slice(0, 4 * TOK), cotv, wave_cols(ring - 1))

    def ring_add(wave, way, part, step):
        ring_wait(wave, way, part, step - 1)
        own = pv[wave, ring_rows(ring_block(way, step)), part * LANE:(part + 1) * LANE]
        total = rv[wave, way, part, step - 1].astype(jnp.float32) + own.astype(jnp.float32)
        rv[wave, way, part, step - 1] = total.astype(jnp.bfloat16)
        ring_next(wave, way, part, step).start()

    def stage_near(wave):
        for way in range(2):
            ring_add(wave, way, way, 1)

    def stage_ring(wave, step):
        for part in range(2):
            for way in range(2):
                ring_add(wave, way, part, step)

    def home_sum(ring):
        for part in range(2):
            for way in range(2):
                ring_wait(ring, way, part, 3)
            lanes = slice(part * LANE, (part + 1) * LANE)
            total = pv[ring, ring_rows(z), lanes].astype(jnp.float32)
            for way in range(2):
                total = total + rv[ring, way, part, 3].astype(jnp.float32)
            pv[ring, ring_rows(z), lanes] = total.astype(jnp.bfloat16)

    def stage_home(ring):
        home_sum(ring)
        pl.when(ring == 0)(lambda: home_half().start())

        @pl.when(ring == 1)
        def _():
            home_half().wait_recv()
            total = pv[1, ring_rows(z), :].astype(jnp.float32) + hx[...].astype(jnp.float32)
            pv[1, ring_rows(z), :] = total.astype(jnp.bfloat16)

        pl.when(ring > 0)(lambda: grad_swap(ring).start())

    def adamw(wave, half, gradient):
        cols = state_cols(wave, half)
        master_now = master_out[:, cols]
        one = beta_one * one_out[:, cols] + (1.0 - beta_one) * gradient
        two = beta_two * two_out[:, cols] + (1.0 - beta_two) * gradient * gradient
        update = one / correct_one / (jnp.sqrt(two / correct_two) + epsilon)
        fresh = master_now - learn_rate * (update + decay_rate * master_now)
        master_out[:, cols] = fresh
        one_out[:, cols] = one
        two_out[:, cols] = two
        wv[half, :, wave_cols(wave)] = fresh.astype(jnp.bfloat16)

    def decode(wave):
        for half in range(2):
            first = half * (SLICES // 2) + 2 * wave
            for which in range(2):
                inputs = jnp.concatenate(
                    [
                        xv[first + part, which].reshape(GROUPS * HROWS, 128)
                        for part in range(2)
                    ],
                    axis=1,
                )
                acc[which] += lax.dot_general(
                    inputs, wv[half, :, wave_cols(wave)], (((1,), (1,)), ((), ())),
                    preferred_element_type=jnp.float32,
                )

    def stage_update(ring):
        wave = ring - 1
        adamw(wave, core, pv[ring, chip_rows(core), :].astype(jnp.float32))
        grad_swap(ring).wait_recv()
        adamw(wave, other, gx[ring].astype(jnp.float32))

    def tick(now, carry):
        def at(moment, *work):
            @pl.when(now == moment)
            def _():
                for part in work:
                    part()

        at(2, lambda: cot_near(2), lambda: hid_begin(1))
        at(3, lambda: cot_far(2), lambda: cot_far(3), cot_end, lambda: hid_begin(2))
        at(7, state_end)

        def each(ring, inner):
            start = START[-1]
            for index in range(RINGS - 1):
                start = jnp.where(ring == index, START[index], start)
            stage = now - start
            home = jnp.where(ring == 1, 6, 4)
            pl.when(stage == 0)(lambda: stage_sum(ring))
            pl.when(stage == 1)(lambda: stage_near(ring))
            pl.when(jnp.logical_or(stage == 2, stage == 3))(
                lambda: stage_ring(ring, stage)
            )
            pl.when(stage == home)(lambda: stage_home(ring))
            pl.when(jnp.logical_and(stage == home + 1, ring > 0))(
                lambda: stage_update(ring)
            )
            return inner

        lax.fori_loop(0, RINGS, each, 0)
        at(0, lambda: cot_begin(2), lambda: cot_near(0), lambda: dec_begin())
        at(1, lambda: cot_begin(3), lambda: cot_near(1), lambda: cot_far(0), lambda: dec_own())
        at(2, lambda: cot_near(3), lambda: cot_far(1))
        at(3, lambda: hid_begin(3), lambda: dec_step(0))
        at(5, lambda: dec_step(1), lambda: dec_cross(7, 0, 3))
        at(6, lambda: dec_step(2))
        at(7, lambda: dec_last(), lambda: dec_cross(1, 4))
        at(8, lambda: dec_cross(2, 5, 6))
        at(9, lambda: dec_end(), lambda: decode(0), lambda: decode(1), lambda: decode(2))
        at(10, lambda: decode(3))
        return carry

    lax.fori_loop(0, LAST + 1, tick, 0)

    def own_rows(group):
        rows = pl.ds(aligned(group * HROWS, HROWS), HROWS)
        return acc[0, rows, :], acc[1, rows, :]

    for offset in range(1, GROUPS):
        group = lax.rem(grp + offset, GROUPS)
        dsend[group] = jnp.concatenate(own_rows(group), axis=0).T.astype(jnp.bfloat16)
        partial_out(offset).start()

    cot_sibling().wait_send()
    cotx_sibling().wait_send()
    home_half().wait_send()
    hid_sibling().wait_send()
    for index in range(4):
        for which in range(2):
            stays = dec_target(index, which) == shard
            pl.when(jnp.logical_not(stays))(lambda: dec_away(index, which).wait_send())
    for offset in range(1, GROUPS):
        dec_pick(offset).wait_send()
    for piece in range(PIECES):
        cot_cross(piece).wait_send()
        for way in range(2):
            cot_y(way, piece).wait_send()
            cot_forward(way, piece).wait_send()
        for which in range(4):
            cot_share(which, piece).wait_send()
    for way in range(2):
        for step in range(4):
            dec_z(way, step).wait_send()
    for slot in range(8):
        dec_half(slot).wait_send()
        for part in range(2):
            dec_share(part, slot).wait_send()

    def drain(ring, carry):
        for way in range(2):
            for part in range(2):
                for step in range(0 if way == part else 1, 4):
                    ring_own(ring, way, part, step).wait_send()

        @pl.when(ring > 0)
        def _():
            grad_swap(ring).wait_send()

        @pl.when(ring > 1)
        def _():
            for target in range(2):
                hid_half(ring - 1, target).wait_send()

        return carry

    lax.fori_loop(0, RINGS, drain, 0)

    total = jnp.concatenate(own_rows(grp), axis=0).T
    for offset in range(1, GROUPS):
        partial_out(offset).wait_recv()
        total = total + drecv[offset].astype(jnp.float32)
    dec_out[...] = total.astype(jnp.bfloat16)
    for offset in range(1, GROUPS):
        partial_out(offset).wait_send()


def body(hidden_acts, cotangent, master, moment_one, moment_two, held_bucket, decode_in):
    any_spec = pl.BlockSpec(memory_space=pl.ANY)
    vmem = pltpu.VMEM
    sems = pltpu.SemaphoreType.DMA
    bf16, f32 = jnp.bfloat16, jnp.float32
    pairs = [
        (3,), (PIECES,), (2, PIECES), (2, PIECES), (4, PIECES), (WAVES, 2), (8,),
        (2, 4), (2, 8), (RINGS, 2, 2, 4), (RINGS,), (1,),
    ]
    both = [sems(shape) for shape in pairs for _ in range(2)]
    *states, decoded = pl.pallas_call(
        kernel,
        out_shape=(pltpu.VMEM((OWN, BUCKET), f32),) * 3 + (vmem((OWN, ROWS), bf16),),
        in_specs=[any_spec] * 5 + [pl.BlockSpec(memory_space=pltpu.SMEM), any_spec],
        out_specs=(pl.BlockSpec(memory_space=pltpu.VMEM),) * 4,
        scratch_shapes=[
            vmem((4 * TOK, HALF), bf16),
            vmem((2 * TOK, HALF), bf16),
            vmem((4 * TOK, COLS), bf16),
            vmem((RINGS, HALF, WCOL), bf16),
            vmem((RINGS, 2, 2, 4, CHIP, LANE), bf16),
            vmem((RINGS, OWN, WCOL), bf16),
            vmem((CHIP, WCOL), bf16),
            vmem((2, OWN, COLS), bf16),
            vmem((GROUPS, HROWS, 128), bf16),
            vmem((GROUPS, HROWS, 128), bf16),
            vmem((SLICES, 2, GROUPS, HROWS, 128), bf16),
            vmem((2, GROUPS * HROWS, OWN), f32),
            vmem((GROUPS, OWN, ROWS), bf16),
            vmem((GROUPS, OWN, ROWS), bf16),
            sems((6,)),
            sems((GROUPS,)),
            *both,
            sems((4, 2)),
            *[sems((GROUPS,)) for _ in range(4)],
        ],
        compiler_params=pltpu.CompilerParams(
            collective_id=0, has_side_effects=True, vmem_limit_bytes=58 * 2**20
        ),
        cost_estimate=pl.CostEstimate(
            flops=12_000_000_000, bytes_accessed=30_000_000, transcendentals=0
        ),
    )(hidden_acts, cotangent, master, moment_one, moment_two, held_bucket, decode_in)
    return (*states, decoded.T)


def solution(mesh):
    placed = (
        P("shard", "grp"),
        P("shard", None),
        P("shard", "grp"),
        P("shard", "grp"),
        P("shard", "grp"),
        P(),
        P("grp", "shard"),
    )
    return jax.shard_map(
        body,
        mesh=mesh,
        in_specs=placed,
        out_specs=(P("shard", "grp"), P("shard", "grp"), P("shard", "grp"), P("grp", "shard")),
        check_vma=False,
    )
```

```python
import jax
import jax.numpy as jnp
from jax import lax
from jax.experimental import pallas as pl
from jax.experimental.pallas import tpu as pltpu
from jax.sharding import PartitionSpec as P

beta_one = 0.9
beta_two = 0.95
learn_rate = 0.001
decay_rate = 0.1
epsilon = 1e-08
correct_one = 1.0 - 0.9**50
correct_two = 1.0 - 0.95**50

NX, NY, NZ = 4, 4, 8
FEAT = 5120
HALF = FEAT // 2
OWN = 160
CHIP = 2 * OWN
TOK = 512
BUCKET = 2048
COLS = BUCKET // 2
WAVES = 4
WCOL = COLS // WAVES
LANE = WCOL // 2
PIECES = 4
PCOL = HALF // PIECES
PROW = TOK // NY
ROWS = 128
DCOL = 512
RINGS = WAVES + 1
START = (0, 1, 3, 4, 5)
LAST = START[-1] + 5
GROUPS = 8
HROWS = ROWS // 2
SLICES = 16


def aligned(value, step):
    return pl.multiple_of(value, step)


def device_at(x, y, z, core):
    x, y, z = lax.rem(x, NX), lax.rem(y, NY), lax.rem(z, NZ)
    return {
        "grp": lax.rem(x, 2) * NY + y,
        "shard": (x // 2) * 16 + z * 2 + core,
    }


def kernel(
    hid, cot, master, mom_one, mom_two, held, dec,
    master_out, one_out, two_out, dec_out,
    cotv, cotx, hidv, pv, rv, gx, hx, wv, a2, pick, xv, acc, dsend, drecv,
    local_sem, a_recv, in_send, in_recv,
    cc_send, cc_recv, cy_send, cy_recv, cf_send, cf_recv, cs_send, cs_recv,
    hx_send, hx_recv, xx_send, xx_recv, xz_send, xz_recv, xs_send, xs_recv,
    r_send, r_recv, g_send, g_recv, h_send, h_recv, a_send, p_send, p_recv, d_send, d_recv,
):
    grp = lax.axis_index("grp")
    shard = lax.axis_index("shard")
    x_lo, y = grp // NY, lax.rem(grp, NY)
    x_hi, z, core = shard // 16, lax.rem(shard, 16) // 2, lax.rem(shard, 2)
    x = x_hi * 2 + x_lo
    other = 1 - core

    sibling = device_at(x, y, z, other)
    z_up, z_down = device_at(x, y, z + 1, core), device_at(x, y, z + NZ - 1, core)
    y_up, y_down = device_at(x, y + 1, z, core), device_at(x, y + NY - 1, z, core)
    x_half = device_at(x + 2, y, z, core)
    x_half_other = device_at(x + 2, y, z, other)
    x_cross = device_at(3 - x, y, z, core)
    slot_here = shard // 2
    z_way = (z_up, z_down)
    y_way = (y_up, y_down)

    def remote(src, dst, send, recv, device):
        return pltpu.make_async_remote_copy(
            src_ref=src, dst_ref=dst, send_sem=send, recv_sem=recv,
            device_id=device, device_id_type=pl.DeviceIdType.MESH,
        )

    barrier = pltpu.get_barrier_semaphore()
    partners = (
        sibling, z_up, z_down, y_up, y_down, x_half, x_half_other, x_cross,
    )

    def greet(device):
        pl.semaphore_signal(
            barrier, inc=1, device_id=device, device_id_type=pl.DeviceIdType.MESH
        )

    def peer(offset):
        return {"grp": lax.rem(grp + offset, GROUPS), "shard": shard}

    for partner in partners:
        greet(partner)
    for offset in range(1, GROUPS):
        greet(peer(offset))
    for bucket in range(GROUPS):
        source = bucket * 4 + shard // 8

        @pl.when(source != shard)
        def _():
            greet({"grp": grp, "shard": source})

    keeps_one = jnp.where(lax.rem(shard, 4) == shard // 8, 1, 0)

    mine = pl.ds(aligned(core * TOK, TOK), TOK)
    loads = [
        pltpu.make_async_copy(
            cot.at[:, pl.ds(aligned(x_hi * HALF, HALF), HALF)], cotv.at[mine, :],
            local_sem.at[0],
        ),
        pltpu.make_async_copy(
            hid.at[:, pl.ds(aligned(core * COLS, COLS), COLS)], hidv.at[mine, :],
            local_sem.at[1],
        ),
        pltpu.make_async_copy(master, master_out, local_sem.at[2]),
        pltpu.make_async_copy(mom_one, one_out, local_sem.at[3]),
        pltpu.make_async_copy(mom_two, two_out, local_sem.at[4]),
        pltpu.make_async_copy(
            cot.at[:, pl.ds(aligned((1 - x_hi) * HALF, HALF), HALF)], cotx.at[mine, :],
            local_sem.at[5],
        ),
    ]
    for index in (1, 5, 0):
        loads[index].start()

    def cot_sibling():
        return remote(
            cot.at[:, pl.ds(aligned(x_hi * HALF, HALF), HALF)], cotv.at[mine, :],
            in_send.at[0], in_recv.at[0], sibling,
        )

    def cotx_sibling():
        return remote(
            cot.at[:, pl.ds(aligned((1 - x_hi) * HALF, HALF), HALF)], cotx.at[mine, :],
            in_send.at[2], in_recv.at[2], sibling,
        )

    def hid_sibling():
        return remote(
            hid.at[:, pl.ds(aligned(other * COLS, COLS), COLS)], hidv.at[mine, :],
            in_send.at[1], in_recv.at[1], sibling,
        )

    def cot_rows(owner, first, count):
        return pl.ds(aligned((2 + core) * TOK + owner * PROW + first, 64), count)

    def cot_cols(piece):
        return pl.ds(aligned(piece * PCOL, PCOL), PCOL)

    def cot_cross(piece):
        return remote(
            cot.at[
                pl.ds(aligned(y * PROW, PROW), PROW),
                pl.ds(aligned((1 - x_hi) * HALF + piece * PCOL, 128), PCOL),
            ],
            cotv.at[cot_rows(y, 0, PROW), cot_cols(piece)],
            cc_send.at[piece], cc_recv.at[piece], x_cross,
        )

    def cot_y(way, piece):
        part = cotv.at[cot_rows(y, 0, PROW), cot_cols(piece)]
        return remote(
            part, part, cy_send.at[way, piece], cy_recv.at[way, piece], y_way[way]
        )

    def cot_forward(way, piece):
        owner = lax.rem(y + (NY - 1 if way == 0 else 1), NY)
        part = cotv.at[cot_rows(owner, way * (PROW // 2), PROW // 2), cot_cols(piece)]
        return remote(
            part, part, cf_send.at[way, piece], cf_recv.at[way, piece], y_way[way]
        )

    def cot_share(piece):
        part = cotv.at[cot_rows(0, 0, TOK), cot_cols(piece)]
        return remote(part, part, cs_send.at[piece], cs_recv.at[piece], sibling)

    def wave_cols(wave):
        return pl.ds(aligned(wave * WCOL, WCOL), WCOL)

    def hid_half(wave, target):
        rows = pl.ds(aligned((2 + core) * TOK, TOK), TOK)
        device = device_at(x + 2, y, z, target)
        return remote(
            hid.at[:, pl.ds(aligned(target * COLS + wave * WCOL, WCOL), WCOL)],
            hidv.at[rows, wave_cols(wave)],
            hx_send.at[wave, target], hx_recv.at[wave, core], device,
        )

    def hid_half_wait(wave, source):
        part = hidv.at[pl.ds((2 + source) * TOK, TOK), wave_cols(wave)]
        pltpu.make_async_copy(part, part, hx_recv.at[wave, source]).wait()

    def dec_target(index, which):
        return (lax.rem(shard, 4) * 4 + index) * 2 + which

    def dec_slice(index, which):
        return dec.at[pl.ds(which * HROWS, HROWS), pl.ds(index * 128, 128)]

    def dec_away(index, which):
        return remote(
            dec_slice(index, which), a2.at[shard // 4],
            a_send.at[index, which], a_recv.at[shard // 4],
            {"grp": grp, "shard": dec_target(index, which)},
        )

    def dec_here(index, which):
        return pltpu.make_async_copy(
            dec_slice(index, which), a2.at[shard // 4], a_recv.at[shard // 4]
        )

    def dec_pick(offset):
        return remote(
            pick.at[lax.rem(grp + offset, GROUPS)], xv.at[slot_here, core, grp],
            p_send.at[offset], p_recv.at[offset], peer(offset),
        )

    def dec_index(half, place):
        return half * 8 + place

    def dec_place(slot):
        shift = (NZ - 1, NZ - 2, NZ - 3, 1, 2, 3, 4, 0)[slot]
        return lax.rem(z + shift, NZ)

    def dec_half(slot):
        block = xv.at[dec_index(x_hi, dec_place(slot)), core]
        return remote(block, block, xx_send.at[slot], xx_recv.at[slot], x_half)

    def dec_z(way, step):
        place = lax.rem(z + (NZ - step if way == 0 else step), NZ)
        groups = pl.ds(0, GROUPS)
        if step == 3:
            groups = pl.ds(way * (GROUPS // 2), GROUPS // 2)
        block = xv.at[dec_index(x_hi, place), core, groups]
        return remote(
            block, block, xz_send.at[way, step], xz_recv.at[way, step], z_way[way]
        )

    def dec_share(part):
        half = x_hi if part == 0 else 1 - x_hi
        block = xv.at[pl.ds(half * 8, 8), core]
        return remote(block, block, xs_send.at[part], xs_recv.at[part], sibling)

    def partial_out(offset):
        return remote(
            dsend.at[lax.rem(grp + offset, GROUPS)], drecv.at[offset],
            d_send.at[offset], d_recv.at[offset], peer(offset),
        )

    def ring_block(way, step):
        if way == 0:
            return lax.rem(z + 4 - step, NZ)
        return lax.rem(z + 4 + step, NZ)

    def ring_rows(place):
        return pl.ds(aligned(place * CHIP, CHIP), CHIP)

    def ring_own(wave, way, part, step):
        return remote(
            pv.at[wave, ring_rows(ring_block(way, step)), pl.ds(part * LANE, LANE)],
            rv.at[wave, way, part, step],
            r_send.at[wave, way, part, step], r_recv.at[wave, way, part, step],
            z_way[way],
        )

    def ring_next(wave, way, part, step):
        return remote(
            rv.at[wave, way, part, step - 1], rv.at[wave, way, part, step],
            r_send.at[wave, way, part, step], r_recv.at[wave, way, part, step],
            z_way[way],
        )

    def ring_wait(wave, way, part, step):
        block = rv.at[wave, way, part, step]
        pltpu.make_async_copy(block, block, r_recv.at[wave, way, part, step]).wait()

    def chip_rows(which):
        return pl.ds(aligned(z * CHIP + which * OWN, 32), OWN)

    def grad_swap(wave):
        return remote(
            pv.at[wave, chip_rows(other), :], gx.at[wave],
            g_send.at[wave], g_recv.at[wave], sibling,
        )

    def home_half():
        return remote(
            pv.at[0, ring_rows(z), :], hx, h_send.at[0], h_recv.at[0], x_half
        )

    def state_cols(wave, half):
        return pl.ds(aligned(half * COLS + wave * WCOL, WCOL), WCOL)

    pl.semaphore_wait(barrier, len(partners) + GROUPS - 1 + GROUPS - keeps_one)
    for piece in range(PIECES):
        cot_cross(piece).start()
    for index in range(4):
        for which in range(2):
            stays = dec_target(index, which) == shard
            pl.when(jnp.logical_not(stays))(lambda: dec_away(index, which).start())
            pl.when(stays)(lambda: dec_here(index, which).start())
    hid_sibling().start()
    cotx_sibling().start()
    cot_sibling().start()

    def dec_begin():
        for bucket in range(GROUPS):
            part = a2.at[bucket]
            pltpu.make_async_copy(part, part, a_recv.at[bucket]).wait()
        for offset in range(1, GROUPS):
            target = lax.rem(grp + offset, GROUPS)
            pick[target] = a2[held[target]]
            dec_pick(offset).start()
        xv[slot_here, core, grp] = a2[held[grp]]

    def dec_own():
        for offset in range(1, GROUPS):
            dec_pick(offset).wait_recv()
        for way in range(2):
            dec_z(way, 0).start()
        dec_half(7).start()

    def dec_step(step):
        for way in range(2):
            dec_z(way, step).wait_recv()
            dec_z(way, step + 1).start()
            dec_half(way * 3 + step).start()

    def dec_last():
        for way in range(2):
            dec_z(way, 3).wait_recv()
        dec_half(6).start()
        dec_share(0).start()

    def dec_cross(*slots):
        for slot in slots:
            dec_half(slot).wait_recv()

    def cot_near(piece):
        for way in range(2):
            cot_y(way, piece).wait_recv()
            cot_forward(way, piece).start()

    def cot_far(piece):
        for way in range(2):
            cot_forward(way, piece).wait_recv()
        cot_share(piece).start()

    def cot_begin(piece):
        cot_cross(piece).wait_recv()
        for way in range(2):
            cot_y(way, piece).start()

    def cot_end():
        for piece in range(PIECES):
            cot_share(piece).wait_recv()

    def state_begin():
        for which in range(3):
            loads[2 + which].start()

    def state_end():
        for which in range(3):
            loads[2 + which].wait()

    def dec_end():
        for part in range(2):
            dec_share(part).wait_recv()

    def hid_begin(wave):
        for target in range(2):
            hid_half(wave, target).start()

    acc[...] = jnp.zeros_like(acc)
    cot_begin(0)
    cot_begin(1)
    loads[1].wait()
    loads[5].wait()
    hid_sibling().wait_recv()
    cotx_sibling().wait_recv()

    def multiply(ring, rows, left, cols):
        def tile(index, carry):
            part = pl.ds(aligned(index * PCOL, PCOL), PCOL)
            value = lax.dot_general(
                left[rows, part], hidv[rows, cols],
                (((0,), (0,)), ((), ())), preferred_element_type=jnp.float32,
            )
            pv[ring, part, :] = value.astype(jnp.bfloat16)
            return carry

        lax.fori_loop(0, PIECES, tile, 0)
        for way in range(2):
            ring_own(ring, way, way, 0).start()
        for way in range(2):
            ring_own(ring, way, 1 - way, 1).start()

    def stage_sum(ring):
        pl.when(ring == 0)(
            lambda: multiply(0, slice(0, 2 * TOK), cotx, slice(0, WCOL))
        )

        @pl.when(ring == 1)
        def _():
            loads[0].wait()
            cot_sibling().wait_recv()
            multiply(1, slice(0, 2 * TOK), cotv, slice(0, WCOL))

        @pl.when(ring > 1)
        def _():
            for source in range(2):
                hid_half_wait(ring - 1, source)
            multiply(ring, slice(0, 4 * TOK), cotv, wave_cols(ring - 1))

    def ring_add(wave, way, part, step):
        ring_wait(wave, way, part, step - 1)
        own = pv[wave, ring_rows(ring_block(way, step)), part * LANE:(part + 1) * LANE]
        total = rv[wave, way, part, step - 1].astype(jnp.float32) + own.astype(jnp.float32)
        rv[wave, way, part, step - 1] = total.astype(jnp.bfloat16)
        ring_next(wave, way, part, step).start()

    def stage_near(wave):
        for way in range(2):
            ring_add(wave, way, way, 1)

    def stage_ring(wave, step):
        for part in range(2):
            for way in range(2):
                ring_add(wave, way, part, step)

    def home_sum(ring):
        for part in range(2):
            for way in range(2):
                ring_wait(ring, way, part, 3)
            lanes = slice(part * LANE, (part + 1) * LANE)
            total = pv[ring, ring_rows(z), lanes].astype(jnp.float32)
            for way in range(2):
                total = total + rv[ring, way, part, 3].astype(jnp.float32)
            pv[ring, ring_rows(z), lanes] = total.astype(jnp.bfloat16)

    def stage_home(ring):
        home_sum(ring)
        pl.when(ring == 0)(lambda: home_half().start())

        @pl.when(ring == 1)
        def _():
            home_half().wait_recv()
            total = pv[1, ring_rows(z), :].astype(jnp.float32) + hx[...].astype(jnp.float32)
            pv[1, ring_rows(z), :] = total.astype(jnp.bfloat16)

        pl.when(ring > 0)(lambda: grad_swap(ring).start())

    def adamw(wave, half, gradient):
        cols = state_cols(wave, half)
        master_now = master_out[:, cols]
        one = beta_one * one_out[:, cols] + (1.0 - beta_one) * gradient
        two = beta_two * two_out[:, cols] + (1.0 - beta_two) * gradient * gradient
        update = one / correct_one / (jnp.sqrt(two / correct_two) + epsilon)
        fresh = master_now - learn_rate * (update + decay_rate * master_now)
        master_out[:, cols] = fresh
        one_out[:, cols] = one
        two_out[:, cols] = two
        wv[half, :, wave_cols(wave)] = fresh.astype(jnp.bfloat16)

    def decode(wave):
        for half in range(2):
            first = half * (SLICES // 2) + 2 * wave
            for which in range(2):
                inputs = jnp.concatenate(
                    [
                        xv[first + part, which].reshape(GROUPS * HROWS, 128)
                        for part in range(2)
                    ],
                    axis=1,
                )
                acc[which] += lax.dot_general(
                    inputs, wv[half, :, wave_cols(wave)], (((1,), (1,)), ((), ())),
                    preferred_element_type=jnp.float32,
                )

    def stage_update(ring):
        wave = ring - 1
        adamw(wave, core, pv[ring, chip_rows(core), :].astype(jnp.float32))
        grad_swap(ring).wait_recv()
        adamw(wave, other, gx[ring].astype(jnp.float32))

    def tick(now, carry):
        def at(moment, *work):
            @pl.when(now == moment)
            def _():
                for part in work:
                    part()

        at(2, lambda: cot_near(2), lambda: hid_begin(1))
        at(3, lambda: cot_far(2), lambda: cot_far(3), cot_end, lambda: hid_begin(2))
        at(7, state_end)

        def each(ring, inner):
            stage = now - START[ring]
            home = (6 if ring == 1 else 4)
            pl.when(stage == 0)(lambda: stage_sum(ring))
            pl.when(stage == 1)(lambda: stage_near(ring))
            pl.when(stage in (2, 3))(
                lambda: stage_ring(ring, stage)
            )
            pl.when(stage == home)(lambda: stage_home(ring))
            pl.when(stage == home + 1 and ring > 0)(
                lambda: stage_update(ring)
            )
            return inner

        for ring in range(RINGS):
            each(ring, 0)
        at(0, lambda: cot_begin(2), lambda: cot_near(0), lambda: dec_begin())
        at(1, lambda: cot_begin(3), lambda: cot_near(1), lambda: cot_far(0), lambda: dec_own())
        at(2, lambda: cot_near(3), lambda: cot_far(1), state_begin)
        at(3, lambda: hid_begin(3), lambda: dec_step(0))
        at(5, lambda: dec_step(1), lambda: dec_cross(7, 0, 3))
        at(6, lambda: dec_step(2))
        at(7, lambda: dec_last(), lambda: dec_cross(1, 4))
        at(8, lambda: dec_cross(2, 5, 6), lambda: dec_share(1).start())
        at(9, lambda: dec_end(), lambda: decode(0), lambda: decode(1), lambda: decode(2))
        at(10, lambda: decode(3))
        return carry

    for now in range(LAST + 1):
        tick(now, 0)

    def own_rows(group):
        rows = pl.ds(aligned(group * HROWS, HROWS), HROWS)
        return acc[0, rows, :], acc[1, rows, :]

    for offset in range(1, GROUPS):
        group = lax.rem(grp + offset, GROUPS)
        dsend[group] = jnp.concatenate(own_rows(group), axis=0).T.astype(jnp.bfloat16)
        partial_out(offset).start()

    cot_sibling().wait_send()
    cotx_sibling().wait_send()
    home_half().wait_send()
    hid_sibling().wait_send()
    for index in range(4):
        for which in range(2):
            stays = dec_target(index, which) == shard
            pl.when(jnp.logical_not(stays))(lambda: dec_away(index, which).wait_send())
    for offset in range(1, GROUPS):
        dec_pick(offset).wait_send()
    for piece in range(PIECES):
        cot_cross(piece).wait_send()
        for way in range(2):
            cot_y(way, piece).wait_send()
            cot_forward(way, piece).wait_send()
        cot_share(piece).wait_send()
    for way in range(2):
        for step in range(4):
            dec_z(way, step).wait_send()
    for slot in range(8):
        dec_half(slot).wait_send()
    for part in range(2):
        dec_share(part).wait_send()

    def drain(ring, carry):
        for way in range(2):
            for part in range(2):
                for step in range(0 if way == part else 1, 4):
                    ring_own(ring, way, part, step).wait_send()

        @pl.when(ring > 0)
        def _():
            grad_swap(ring).wait_send()

        @pl.when(ring > 1)
        def _():
            for target in range(2):
                hid_half(ring - 1, target).wait_send()

        return carry

    lax.fori_loop(0, RINGS, drain, 0)

    total = jnp.concatenate(own_rows(grp), axis=0).T
    for offset in range(1, GROUPS):
        partial_out(offset).wait_recv()
        total = total + drecv[offset].astype(jnp.float32)
    dec_out[...] = total.astype(jnp.bfloat16)
    for offset in range(1, GROUPS):
        partial_out(offset).wait_send()


def body(hidden_acts, cotangent, master, moment_one, moment_two, held_bucket, decode_in):
    any_spec = pl.BlockSpec(memory_space=pl.ANY)
    vmem = pltpu.VMEM
    sems = pltpu.SemaphoreType.DMA
    bf16, f32 = jnp.bfloat16, jnp.float32
    pairs = [
        (3,), (PIECES,), (2, PIECES), (2, PIECES), (PIECES,), (WAVES, 2), (8,),
        (2, 4), (2,), (RINGS, 2, 2, 4), (RINGS,), (1,),
    ]
    both = [sems(shape) for shape in pairs for _ in range(2)]
    *states, decoded = pl.pallas_call(
        kernel,
        out_shape=(pltpu.VMEM((OWN, BUCKET), f32),) * 3 + (vmem((OWN, ROWS), bf16),),
        in_specs=[any_spec] * 5 + [pl.BlockSpec(memory_space=pltpu.SMEM), any_spec],
        out_specs=(pl.BlockSpec(memory_space=pltpu.VMEM),) * 4,
        scratch_shapes=[
            vmem((4 * TOK, HALF), bf16),
            vmem((2 * TOK, HALF), bf16),
            vmem((4 * TOK, COLS), bf16),
            vmem((RINGS, HALF, WCOL), bf16),
            vmem((RINGS, 2, 2, 4, CHIP, LANE), bf16),
            vmem((RINGS, OWN, WCOL), bf16),
            vmem((CHIP, WCOL), bf16),
            vmem((2, OWN, COLS), bf16),
            vmem((GROUPS, HROWS, 128), bf16),
            vmem((GROUPS, HROWS, 128), bf16),
            vmem((SLICES, 2, GROUPS, HROWS, 128), bf16),
            vmem((2, GROUPS * HROWS, OWN), f32),
            vmem((GROUPS, OWN, ROWS), bf16),
            vmem((GROUPS, OWN, ROWS), bf16),
            sems((6,)),
            sems((GROUPS,)),
            *both,
            sems((4, 2)),
            *[sems((GROUPS,)) for _ in range(4)],
        ],
        compiler_params=pltpu.CompilerParams(
            collective_id=0, has_side_effects=True, vmem_limit_bytes=58 * 2**20
        ),
        cost_estimate=pl.CostEstimate(
            flops=12_000_000_000, bytes_accessed=30_000_000, transcendentals=0
        ),
    )(hidden_acts, cotangent, master, moment_one, moment_two, held_bucket, decode_in)
    return (*states, decoded.T)


def solution(mesh):
    placed = (
        P("shard", "grp"),
        P("shard", None),
        P("shard", "grp"),
        P("shard", "grp"),
        P("shard", "grp"),
        P(),
        P("grp", "shard"),
    )
    return jax.shard_map(
        body,
        mesh=mesh,
        in_specs=placed,
        out_specs=(P("shard", "grp"), P("shard", "grp"), P("shard", "grp"), P("grp", "shard")),
        check_vma=False,
    )
```

```python
import jax
import jax.numpy as jnp
from jax import lax
from jax.experimental import pallas as pl
from jax.experimental.pallas import tpu as pltpu
from jax.sharding import PartitionSpec as P

beta_one = 0.9
beta_two = 0.95
learn_rate = 0.001
decay_rate = 0.1
epsilon = 1e-08
correct_one = 1.0 - 0.9**50
correct_two = 1.0 - 0.95**50

NX, NY, NZ = 4, 4, 8
FEAT = 5120
HALF = FEAT // 2
OWN = 160
CHIP = 2 * OWN
TOK = 512
BUCKET = 2048
COLS = BUCKET // 2
WAVES = 4
WCOL = COLS // WAVES
LANE = WCOL // 2
PIECES = 4
PCOL = HALF // PIECES
PROW = TOK // NY
ROWS = 128
DCOL = 512
RINGS = WAVES + 1
START = (0, 1, 3, 4, 5)
LAST = START[-1] + 5
GROUPS = 8
HROWS = ROWS // 2
SLICES = 16


def aligned(value, step):
    return pl.multiple_of(value, step)


def device_at(x, y, z, core):
    x, y, z = lax.rem(x, NX), lax.rem(y, NY), lax.rem(z, NZ)
    return {
        "grp": lax.rem(x, 2) * NY + y,
        "shard": (x // 2) * 16 + z * 2 + core,
    }


def kernel(
    hid, cot, master, mom_one, mom_two, held, dec,
    master_out, one_out, two_out, dec_out,
    cotv, cotx, hidv, pv, rv, gx, hx, wv, a2, pick, xv, acc, dsend, drecv,
    local_sem, a_recv, in_send, in_recv,
    cc_send, cc_recv, cy_send, cy_recv, cf_send, cf_recv, cs_send, cs_recv,
    hx_send, hx_recv, xx_send, xx_recv, xz_send, xz_recv, xs_send, xs_recv,
    r_send, r_recv, g_send, g_recv, h_send, h_recv, a_send, p_send, p_recv, d_send, d_recv,
):
    grp = lax.axis_index("grp")
    shard = lax.axis_index("shard")
    x_lo, y = grp // NY, lax.rem(grp, NY)
    x_hi, z, core = shard // 16, lax.rem(shard, 16) // 2, lax.rem(shard, 2)
    x = x_hi * 2 + x_lo
    other = 1 - core

    sibling = device_at(x, y, z, other)
    z_up, z_down = device_at(x, y, z + 1, core), device_at(x, y, z + NZ - 1, core)
    y_up, y_down = device_at(x, y + 1, z, core), device_at(x, y + NY - 1, z, core)
    x_half = device_at(x + 2, y, z, core)
    x_half_other = device_at(x + 2, y, z, other)
    x_cross = device_at(3 - x, y, z, core)
    slot_here = shard // 2
    z_way = (z_up, z_down)
    y_way = (y_up, y_down)

    def remote(src, dst, send, recv, device):
        return pltpu.make_async_remote_copy(
            src_ref=src, dst_ref=dst, send_sem=send, recv_sem=recv,
            device_id=device, device_id_type=pl.DeviceIdType.MESH,
        )

    barrier = pltpu.get_barrier_semaphore()
    partners = (
        sibling, z_up, z_down, y_up, y_down, x_half, x_half_other, x_cross,
    )

    def greet(device):
        pl.semaphore_signal(
            barrier, inc=1, device_id=device, device_id_type=pl.DeviceIdType.MESH
        )

    def peer(offset):
        return {"grp": lax.rem(grp + offset, GROUPS), "shard": shard}

    for partner in partners:
        greet(partner)
    for offset in range(1, GROUPS):
        greet(peer(offset))
    for bucket in range(GROUPS):
        source = bucket * 4 + shard // 8

        @pl.when(source != shard)
        def _():
            greet({"grp": grp, "shard": source})

    keeps_one = jnp.where(lax.rem(shard, 4) == shard // 8, 1, 0)

    mine = pl.ds(aligned(core * TOK, TOK), TOK)
    loads = [
        pltpu.make_async_copy(
            cot.at[:, pl.ds(aligned(x_hi * HALF, HALF), HALF)], cotv.at[mine, :],
            local_sem.at[0],
        ),
        pltpu.make_async_copy(
            hid.at[:, pl.ds(aligned(core * COLS, COLS), COLS)], hidv.at[mine, :],
            local_sem.at[1],
        ),
        pltpu.make_async_copy(master, master_out, local_sem.at[2]),
        pltpu.make_async_copy(mom_one, one_out, local_sem.at[3]),
        pltpu.make_async_copy(mom_two, two_out, local_sem.at[4]),
        pltpu.make_async_copy(
            cot.at[:, pl.ds(aligned((1 - x_hi) * HALF, HALF), HALF)], cotx.at[mine, :],
            local_sem.at[5],
        ),
    ]
    for index in (1, 5, 0):
        loads[index].start()

    def cot_sibling():
        return remote(
            cot.at[:, pl.ds(aligned(x_hi * HALF, HALF), HALF)], cotv.at[mine, :],
            in_send.at[0], in_recv.at[0], sibling,
        )

    def cotx_sibling():
        return remote(
            cot.at[:, pl.ds(aligned((1 - x_hi) * HALF, HALF), HALF)], cotx.at[mine, :],
            in_send.at[2], in_recv.at[2], sibling,
        )

    def hid_sibling():
        return remote(
            hid.at[:, pl.ds(aligned(other * COLS, COLS), COLS)], hidv.at[mine, :],
            in_send.at[1], in_recv.at[1], sibling,
        )

    def cot_rows(owner, first, count):
        return pl.ds(aligned((2 + core) * TOK + owner * PROW + first, 64), count)

    def cot_cols(piece):
        return pl.ds(aligned(piece * PCOL, PCOL), PCOL)

    def cot_cross(piece):
        return remote(
            cot.at[
                pl.ds(aligned(y * PROW, PROW), PROW),
                pl.ds(aligned((1 - x_hi) * HALF + piece * PCOL, 128), PCOL),
            ],
            cotv.at[cot_rows(y, 0, PROW), cot_cols(piece)],
            cc_send.at[piece], cc_recv.at[piece], x_cross,
        )

    def cot_y(way, piece):
        part = cotv.at[cot_rows(y, 0, PROW), cot_cols(piece)]
        return remote(
            part, part, cy_send.at[way, piece], cy_recv.at[way, piece], y_way[way]
        )

    def cot_forward(way, piece):
        owner = lax.rem(y + (NY - 1 if way == 0 else 1), NY)
        part = cotv.at[cot_rows(owner, way * (PROW // 2), PROW // 2), cot_cols(piece)]
        return remote(
            part, part, cf_send.at[way, piece], cf_recv.at[way, piece], y_way[way]
        )

    def cot_share(piece):
        part = cotv.at[cot_rows(0, 0, TOK), cot_cols(piece)]
        return remote(part, part, cs_send.at[piece], cs_recv.at[piece], sibling)

    def wave_cols(wave):
        return pl.ds(aligned(wave * WCOL, WCOL), WCOL)

    def hid_half(wave, target):
        rows = pl.ds(aligned((2 + core) * TOK, TOK), TOK)
        device = device_at(x + 2, y, z, target)
        return remote(
            hid.at[:, pl.ds(aligned(target * COLS + wave * WCOL, WCOL), WCOL)],
            hidv.at[rows, wave_cols(wave)],
            hx_send.at[wave, target], hx_recv.at[wave, core], device,
        )

    def hid_half_wait(wave, source):
        part = hidv.at[pl.ds((2 + source) * TOK, TOK), wave_cols(wave)]
        pltpu.make_async_copy(part, part, hx_recv.at[wave, source]).wait()

    def dec_target(index, which):
        return (lax.rem(shard, 4) * 4 + index) * 2 + which

    def dec_slice(index, which):
        return dec.at[pl.ds(which * HROWS, HROWS), pl.ds(index * 128, 128)]

    def dec_away(index, which):
        return remote(
            dec_slice(index, which), a2.at[shard // 4],
            a_send.at[index, which], a_recv.at[shard // 4],
            {"grp": grp, "shard": dec_target(index, which)},
        )

    def dec_here(index, which):
        return pltpu.make_async_copy(
            dec_slice(index, which), a2.at[shard // 4], a_recv.at[shard // 4]
        )

    def dec_pick(offset):
        return remote(
            pick.at[lax.rem(grp + offset, GROUPS)], xv.at[slot_here, core, grp],
            p_send.at[offset], p_recv.at[offset], peer(offset),
        )

    def dec_index(half, place):
        return half * 8 + place

    def dec_place(slot):
        shift = (NZ - 1, NZ - 2, NZ - 3, 1, 2, 3, 4, 0)[slot]
        return lax.rem(z + shift, NZ)

    def dec_half(slot):
        block = xv.at[dec_index(x_hi, dec_place(slot)), core]
        return remote(block, block, xx_send.at[slot], xx_recv.at[slot], x_half)

    def dec_z(way, step):
        place = lax.rem(z + (NZ - step if way == 0 else step), NZ)
        groups = pl.ds(0, GROUPS)
        if step == 3:
            groups = pl.ds(way * (GROUPS // 2), GROUPS // 2)
        block = xv.at[dec_index(x_hi, place), core, groups]
        return remote(
            block, block, xz_send.at[way, step], xz_recv.at[way, step], z_way[way]
        )

    def dec_share(part):
        half = x_hi if part == 0 else 1 - x_hi
        block = xv.at[pl.ds(half * 8, 8), core]
        return remote(block, block, xs_send.at[part], xs_recv.at[part], sibling)

    def partial_out(offset):
        return remote(
            dsend.at[lax.rem(grp + offset, GROUPS)], drecv.at[offset],
            d_send.at[offset], d_recv.at[offset], peer(offset),
        )

    def ring_block(way, step):
        if way == 0:
            return lax.rem(z + 4 - step, NZ)
        return lax.rem(z + 4 + step, NZ)

    def ring_rows(place):
        return pl.ds(aligned(place * CHIP, CHIP), CHIP)

    def ring_own(wave, way, part, step):
        return remote(
            pv.at[wave, ring_rows(ring_block(way, step)), pl.ds(part * LANE, LANE)],
            rv.at[wave, way, part, step],
            r_send.at[wave, way, part, step], r_recv.at[wave, way, part, step],
            z_way[way],
        )

    def ring_next(wave, way, part, step):
        return remote(
            rv.at[wave, way, part, step - 1], rv.at[wave, way, part, step],
            r_send.at[wave, way, part, step], r_recv.at[wave, way, part, step],
            z_way[way],
        )

    def ring_wait(wave, way, part, step):
        block = rv.at[wave, way, part, step]
        pltpu.make_async_copy(block, block, r_recv.at[wave, way, part, step]).wait()

    def chip_rows(which):
        return pl.ds(aligned(z * CHIP + which * OWN, 32), OWN)

    def grad_swap(wave):
        return remote(
            pv.at[wave, chip_rows(other), :], gx.at[wave],
            g_send.at[wave], g_recv.at[wave], sibling,
        )

    def home_half():
        return remote(
            pv.at[0, ring_rows(z), :], hx, h_send.at[0], h_recv.at[0], x_half
        )

    def state_cols(wave, half):
        return pl.ds(aligned(half * COLS + wave * WCOL, WCOL), WCOL)

    pl.semaphore_wait(barrier, len(partners) + GROUPS - 1 + GROUPS - keeps_one)
    for piece in range(PIECES):
        cot_cross(piece).start()
    for index in range(4):
        for which in range(2):
            stays = dec_target(index, which) == shard
            pl.when(jnp.logical_not(stays))(lambda: dec_away(index, which).start())
            pl.when(stays)(lambda: dec_here(index, which).start())
    hid_sibling().start()
    cotx_sibling().start()
    cot_sibling().start()

    def dec_begin():
        for bucket in range(GROUPS):
            part = a2.at[bucket]
            pltpu.make_async_copy(part, part, a_recv.at[bucket]).wait()
        for offset in range(1, GROUPS):
            target = lax.rem(grp + offset, GROUPS)
            pick[target] = a2[held[target]]
            dec_pick(offset).start()
        xv[slot_here, core, grp] = a2[held[grp]]

    def dec_own():
        for offset in range(1, GROUPS):
            dec_pick(offset).wait_recv()
        for way in range(2):
            dec_z(way, 0).start()
        dec_half(7).start()

    def dec_step(step):
        for way in range(2):
            dec_z(way, step).wait_recv()
            dec_z(way, step + 1).start()
            dec_half(way * 3 + step).start()

    def dec_last():
        for way in range(2):
            dec_z(way, 3).wait_recv()
        dec_half(6).start()
        dec_share(0).start()

    def dec_cross(*slots):
        for slot in slots:
            dec_half(slot).wait_recv()

    def cot_near(piece):
        for way in range(2):
            cot_y(way, piece).wait_recv()
            cot_forward(way, piece).start()

    def cot_far(piece):
        for way in range(2):
            cot_forward(way, piece).wait_recv()
        cot_share(piece).start()

    def cot_begin(piece):
        cot_cross(piece).wait_recv()
        for way in range(2):
            cot_y(way, piece).start()

    def cot_end():
        for piece in range(PIECES):
            cot_share(piece).wait_recv()

    def state_begin():
        for which in range(3):
            loads[2 + which].start()

    def state_end():
        for which in range(3):
            loads[2 + which].wait()

    def dec_end():
        for part in range(2):
            dec_share(part).wait_recv()

    def hid_begin(wave):
        for target in range(2):
            hid_half(wave, target).start()

    acc[...] = jnp.zeros_like(acc)
    cot_begin(0)
    cot_begin(1)
    loads[1].wait()
    loads[5].wait()
    hid_sibling().wait_recv()
    cotx_sibling().wait_recv()

    def multiply(ring, rows, left, cols):
        def tile(index, carry):
            part = pl.ds(aligned(index * PCOL, PCOL), PCOL)
            value = lax.dot_general(
                left[rows, part], hidv[rows, cols],
                (((0,), (0,)), ((), ())), preferred_element_type=jnp.float32,
            )
            pv[ring, part, :] = value.astype(jnp.bfloat16)
            return carry

        lax.fori_loop(0, PIECES, tile, 0)
        for way in range(2):
            ring_own(ring, way, way, 0).start()
        for way in range(2):
            ring_own(ring, way, 1 - way, 1).start()

    def stage_sum(ring):
        pl.when(ring == 0)(
            lambda: multiply(0, slice(0, 2 * TOK), cotx, slice(0, WCOL))
        )

        @pl.when(ring == 1)
        def _():
            loads[0].wait()
            cot_sibling().wait_recv()
            multiply(1, slice(0, 2 * TOK), cotv, slice(0, WCOL))

        @pl.when(ring > 1)
        def _():
            for source in range(2):
                hid_half_wait(ring - 1, source)
            multiply(ring, slice(0, 4 * TOK), cotv, wave_cols(ring - 1))

    def ring_add(wave, way, part, step):
        ring_wait(wave, way, part, step - 1)
        own = pv[wave, ring_rows(ring_block(way, step)), part * LANE:(part + 1) * LANE]
        total = rv[wave, way, part, step - 1].astype(jnp.float32) + own.astype(jnp.float32)
        rv[wave, way, part, step - 1] = total.astype(jnp.bfloat16)
        ring_next(wave, way, part, step).start()

    def stage_near(wave):
        for way in range(2):
            ring_add(wave, way, way, 1)

    def stage_ring(wave, step):
        for part in range(2):
            for way in range(2):
                ring_add(wave, way, part, step)

    def home_sum(ring):
        for part in range(2):
            for way in range(2):
                ring_wait(ring, way, part, 3)
            lanes = slice(part * LANE, (part + 1) * LANE)
            total = pv[ring, ring_rows(z), lanes].astype(jnp.float32)
            for way in range(2):
                total = total + rv[ring, way, part, 3].astype(jnp.float32)
            pv[ring, ring_rows(z), lanes] = total.astype(jnp.bfloat16)

    def stage_home(ring):
        home_sum(ring)
        pl.when(ring == 0)(lambda: home_half().start())

        @pl.when(ring == 1)
        def _():
            home_half().wait_recv()
            total = pv[1, ring_rows(z), :].astype(jnp.float32) + hx[...].astype(jnp.float32)
            pv[1, ring_rows(z), :] = total.astype(jnp.bfloat16)

        pl.when(ring > 0)(lambda: grad_swap(ring).start())

    def adamw(wave, half, gradient):
        cols = state_cols(wave, half)
        master_now = master_out[:, cols]
        one = beta_one * one_out[:, cols] + (1.0 - beta_one) * gradient
        two = beta_two * two_out[:, cols] + (1.0 - beta_two) * gradient * gradient
        update = one * (1.0 / correct_one) / (jnp.sqrt(two * (1.0 / correct_two)) + epsilon)
        fresh = master_now - learn_rate * (update + decay_rate * master_now)
        master_out[:, cols] = fresh
        one_out[:, cols] = one
        two_out[:, cols] = two
        wv[half, :, wave_cols(wave)] = fresh.astype(jnp.bfloat16)

    def decode(wave, halves=(0, 1)):
        for half in halves:
            first = half * (SLICES // 2) + 2 * wave
            for which in range(2):
                inputs = jnp.concatenate(
                    [
                        xv[first + part, which].reshape(GROUPS * HROWS, 128)
                        for part in range(2)
                    ],
                    axis=1,
                )
                acc[which] += lax.dot_general(
                    inputs, wv[half, :, wave_cols(wave)], (((1,), (1,)), ((), ())),
                    preferred_element_type=jnp.float32,
                )

    def stage_update(ring):
        wave = ring - 1
        adamw(wave, core, pv[ring, chip_rows(core), :].astype(jnp.float32))
        if ring == RINGS - 1:
            decode(wave, (core,))
        grad_swap(ring).wait_recv()
        adamw(wave, other, gx[ring].astype(jnp.float32))
        if ring == RINGS - 1:
            decode(wave, (other,))

    def tick(now, carry):
        def at(moment, *work):
            @pl.when(now == moment)
            def _():
                for part in work:
                    part()

        at(2, lambda: cot_near(2), lambda: hid_begin(1))
        at(3, lambda: cot_far(2), lambda: cot_far(3), cot_end, lambda: hid_begin(2))
        at(7, state_end)

        def each(ring, inner):
            stage = now - START[ring]
            home = (6 if ring == 1 else 4)
            pl.when(stage == 0)(lambda: stage_sum(ring))
            pl.when(stage == 1)(lambda: stage_near(ring))
            pl.when(stage in (2, 3))(
                lambda: stage_ring(ring, stage)
            )
            pl.when(stage == home)(lambda: stage_home(ring))
            pl.when(stage == home + 1 and ring > 0)(
                lambda: stage_update(ring)
            )
            return inner

        for ring in range(RINGS):
            each(ring, 0)
        at(0, lambda: cot_begin(2), lambda: cot_near(0))
        at(1, lambda: cot_begin(3), lambda: cot_near(1), lambda: cot_far(0), dec_begin)
        at(2, lambda: cot_near(3), lambda: cot_far(1), state_begin)
        at(3, lambda: hid_begin(3), dec_own)
        at(4, lambda: dec_step(0))
        at(5, lambda: dec_step(1))
        at(6, lambda: dec_step(2), lambda: dec_cross(7, 0, 3))
        at(7, lambda: dec_last(), lambda: dec_cross(1, 4))
        at(8, lambda: dec_cross(2, 5, 6), lambda: dec_share(1).start())
        at(9, lambda: dec_end(), lambda: decode(0), lambda: decode(1), lambda: decode(2))
        return carry

    for now in range(LAST + 1):
        tick(now, 0)

    def own_rows(group):
        rows = pl.ds(aligned(group * HROWS, HROWS), HROWS)
        return acc[0, rows, :], acc[1, rows, :]

    for offset in range(1, GROUPS):
        group = lax.rem(grp + offset, GROUPS)
        dsend[group] = jnp.concatenate(own_rows(group), axis=0).T.astype(jnp.bfloat16)
        partial_out(offset).start()

    cot_sibling().wait_send()
    cotx_sibling().wait_send()
    home_half().wait_send()
    hid_sibling().wait_send()
    for index in range(4):
        for which in range(2):
            stays = dec_target(index, which) == shard
            pl.when(jnp.logical_not(stays))(lambda: dec_away(index, which).wait_send())
    for offset in range(1, GROUPS):
        dec_pick(offset).wait_send()
    for piece in range(PIECES):
        cot_cross(piece).wait_send()
        for way in range(2):
            cot_y(way, piece).wait_send()
            cot_forward(way, piece).wait_send()
        cot_share(piece).wait_send()
    for way in range(2):
        for step in range(4):
            dec_z(way, step).wait_send()
    for slot in range(8):
        dec_half(slot).wait_send()
    for part in range(2):
        dec_share(part).wait_send()

    def drain(ring, carry):
        for way in range(2):
            for part in range(2):
                for step in range(0 if way == part else 1, 4):
                    ring_own(ring, way, part, step).wait_send()

        @pl.when(ring > 0)
        def _():
            grad_swap(ring).wait_send()

        @pl.when(ring > 1)
        def _():
            for target in range(2):
                hid_half(ring - 1, target).wait_send()

        return carry

    lax.fori_loop(0, RINGS, drain, 0)

    total = jnp.concatenate(own_rows(grp), axis=0).T
    for offset in range(1, GROUPS):
        partial_out(offset).wait_recv()
        total = total + drecv[offset].astype(jnp.float32)
    dec_out[...] = total.astype(jnp.bfloat16)
    for offset in range(1, GROUPS):
        partial_out(offset).wait_send()


def body(hidden_acts, cotangent, master, moment_one, moment_two, held_bucket, decode_in):
    any_spec = pl.BlockSpec(memory_space=pl.ANY)
    vmem = pltpu.VMEM
    sems = pltpu.SemaphoreType.DMA
    bf16, f32 = jnp.bfloat16, jnp.float32
    pairs = [
        (3,), (PIECES,), (2, PIECES), (2, PIECES), (PIECES,), (WAVES, 2), (8,),
        (2, 4), (2,), (RINGS, 2, 2, 4), (RINGS,), (1,),
    ]
    both = [sems(shape) for shape in pairs for _ in range(2)]
    *states, decoded = pl.pallas_call(
        kernel,
        out_shape=(pltpu.VMEM((OWN, BUCKET), f32),) * 3 + (vmem((OWN, ROWS), bf16),),
        in_specs=[any_spec] * 5 + [pl.BlockSpec(memory_space=pltpu.SMEM), any_spec],
        out_specs=(pl.BlockSpec(memory_space=pltpu.VMEM),) * 4,
        scratch_shapes=[
            vmem((4 * TOK, HALF), bf16),
            vmem((2 * TOK, HALF), bf16),
            vmem((4 * TOK, COLS), bf16),
            vmem((RINGS, HALF, WCOL), bf16),
            vmem((RINGS, 2, 2, 4, CHIP, LANE), bf16),
            vmem((RINGS, OWN, WCOL), bf16),
            vmem((CHIP, WCOL), bf16),
            vmem((2, OWN, COLS), bf16),
            vmem((GROUPS, HROWS, 128), bf16),
            vmem((GROUPS, HROWS, 128), bf16),
            vmem((SLICES, 2, GROUPS, HROWS, 128), bf16),
            vmem((2, GROUPS * HROWS, OWN), f32),
            vmem((GROUPS, OWN, ROWS), bf16),
            vmem((GROUPS, OWN, ROWS), bf16),
            sems((6,)),
            sems((GROUPS,)),
            *both,
            sems((4, 2)),
            *[sems((GROUPS,)) for _ in range(4)],
        ],
        compiler_params=pltpu.CompilerParams(
            collective_id=0, has_side_effects=True, vmem_limit_bytes=58 * 2**20
        ),
        cost_estimate=pl.CostEstimate(
            flops=12_000_000_000, bytes_accessed=30_000_000, transcendentals=0
        ),
    )(hidden_acts, cotangent, master, moment_one, moment_two, held_bucket, decode_in)
    return (*states, decoded.T)


def solution(mesh):
    placed = (
        P("shard", "grp"),
        P("shard", None),
        P("shard", "grp"),
        P("shard", "grp"),
        P("shard", "grp"),
        P(),
        P("grp", "shard"),
    )
    return jax.shard_map(
        body,
        mesh=mesh,
        in_specs=placed,
        out_specs=(P("shard", "grp"), P("shard", "grp"), P("shard", "grp"), P("grp", "shard")),
        check_vma=False,
    )
```
